256 devices in a mesh: dp: 32 (over x, z_lo, core), group: 8 (over y, z_hi).
Axes of the slice: x: 4, y: 4, z: 8 (z_hi: 2, z_lo: 4; z = z_hi * 4 + z_lo), core: 2. Of those that a mesh axis runs over, the one named last changes fastest.
Arguments:
- hidden_act: bfloat16 [32768, 2, 1536], P('dp'), may hold values from -12 to 12
- out_grad: bfloat16 [32768, 2, 4096], P('dp', None, 'group'), may hold values from -0.03125 to 0.03125
- router_grads: float32 [32, 2, 4096], P('dp'), may hold values from -4 to 4
- small_grads: float32 [32, 8192], P('dp'), may hold values from -2 to 2
- expert_ids: int32 [2], replicated, may hold values from 0 to 127, as said below
- small_lengths: int32 [16], replicated, may hold values from 1 to 2048, 8192 in all
- small_rate: float32 [16], replicated, may hold values from 0.25 to 4
- expert_w: float32 [2, 1536, 4096], P(None, 'dp', 'group'), may hold values from -6 to 6
- expert_m: float32 [2, 1536, 4096], P(None, 'dp', 'group'), may hold values from -3 to 3
- expert_v: float32 [2, 1536, 4096], P(None, 'dp', 'group'), may hold values from 0.1 to 4
- router_w: float32 [128, 4096], P(None, 'dp'), may hold values from -6 to 6
- router_m: float32 [128, 4096], P(None, 'dp'), may hold values from -3 to 3
- router_v: float32 [128, 4096], P(None, 'dp'), may hold values from 0.1 to 4
- small_w: float32 [8192], P('dp'), may hold values from 0.5 to 1.5
- small_m: float32 [8192], P('dp'), may hold values from -3 to 3
- small_v: float32 [8192], P('dp'), may hold values from 0.1 to 4
Outputs:
- new_expert: float32 [2, 1536, 4096], P(None, 'dp', 'group')
- expert_moment: float32 [2, 1536, 4096], P(None, 'dp', 'group')
- expert_second: float32 [2, 1536, 4096], P(None, 'dp', 'group')
- new_router: float32 [128, 4096], P(None, 'dp')
- router_moment: float32 [128, 4096], P(None, 'dp')
- router_second: float32 [128, 4096], P(None, 'dp')
- new_small: float32 [8192], P('dp')
- small_moment: float32 [8192], P('dp')
- small_second: float32 [8192], P('dp')
- expert_rollout: bfloat16 [2, 1536, 4096], P(None, 'group')
- router_rollout: bfloat16 [128, 4096], replicated
- small_rollout: bfloat16 [8192], replicated
The draws below stay inside these ranges and needn't reach their ends.
Inputs may be any that keep to these rules, and one draw needn't show every extreme that they name: `expert_ids`: 2 distinct expert numbers below 128, the last expert among them. `small_lengths`: they sum to 8192.
All inputs are finite; a program needn't handle non-finite values.
Results may differ from the reference program's by a relative error of at most 0.009.
Values may be sent and summed in bfloat16 or wider, within the bound.
No kernel may reach another device: no remote copies, remote signals or barrier semaphores. Data moves between devices by JAX's collectives and lax.ppermute only.
A program may use at most 128 MiB of HBM per device.

```python
import math
import jax
import jax.numpy as jnp
import numpy as np
from jax import lax

D = 4096
FF = 1536
NE = 128
EW = 2
NT = 16
TOK_DEV = 1024
TOKENS = 32768
SMALL = 8192
N_DP = 32


def draw_expert_ids(key, part):
    key = jax.random.fold_in(key, 7)
    first_key = jax.random.fold_in(key, 101)
    second_key = jax.random.fold_in(key, 202)
    others_count = NE - 1
    scores = jax.random.randint(first_key, (others_count,), 0, 1 << 20).astype(jnp.int32) * others_count + jnp.arange(others_count, dtype=jnp.int32)
    ranking = jnp.argsort(scores, stable=True).astype(jnp.int32)
    others = ranking[:EW - 1].astype(jnp.int32)
    place = jax.random.randint(second_key, (), 0, EW).astype(jnp.int32)
    slots = jnp.arange(EW, dtype=jnp.int32)
    index_other = jnp.clip(slots - (slots > place).astype(jnp.int32), 0, EW - 2).astype(jnp.int32)
    filled = jnp.concatenate([others, jnp.zeros((1,), jnp.int32)])[index_other]
    return jnp.where(slots == place, jnp.int32(NE - 1), filled).astype(jnp.int32)


def strengthened(entries, own_key, source, target, parts, factor):
    def block_of(position):
        return (jnp.arange(entries.shape[position]) // (entries.shape[position] // parts)).reshape((-1,) + (1,) * (entries.ndim - 1 - position))

    near = jax.random.permutation(own_key, parts)[block_of(target)]
    second = (block_of(target) + parts // 2) % parts
    return jnp.where((block_of(source) == near) | (block_of(source) == second), factor * entries, entries)


def block_scale(rng, extent, pieces, low, high):
    def one(dim, blocks):
        steps = jax.random.uniform(jax.random.fold_in(jax.random.fold_in(rng, 6), dim), (blocks,), jnp.float32, low / len(pieces), high / len(pieces))
        return jnp.repeat(jnp.exp(steps), extent[dim] // blocks).reshape((-1,) + (1,) * (len(extent) - dim - 1))

    gain = one(*pieces[0])
    for cut in pieces[1:]:
        gain = gain * one(*cut)
    return gain


def length_profile(number_of, total, bound, slope):
    portions = [(1 << 20) // math.isqrt(standing ** slope) + 1 for standing in range(2, number_of + 1)]
    spare, given = total - bound - (number_of - 1), [1] * (number_of - 1)
    while spare > 0:
        candidates = [i for i in range(number_of - 1) if given[i] < bound]
        whole, remaining = sum([portions[i] for i in candidates]), spare
        for i in candidates:
            more = min(bound - given[i], max(1, remaining * portions[i] // whole), spare)
            given[i] = given[i] + more
            spare = spare - more
    return np.array([bound] + given)


def uneven(rng, number_of, total, most, lean):
    if number_of == 2:
        one = jax.random.randint(rng, (), max(1, total - most), min(most, total - 1) + 1)
        return jnp.stack([one, total - one])
    sizes = jnp.asarray(length_profile(number_of, total, most, lean), jnp.int32)
    twos = (number_of - 1) // 2
    donor, sink = sizes[1:1 + 2 * twos:2], sizes[2:2 + 2 * twos:2]
    margin = jnp.minimum(donor - 1, most - sink)
    shifted = jax.random.randint(jax.random.fold_in(rng, 1), (twos,), 0, 1 << 20) % (margin + 1)
    sizes = sizes.at[1:1 + 2 * twos:2].set(donor - shifted).at[2:2 + 2 * twos:2].set(sink + shifted)
    return sizes[jax.random.permutation(jax.random.fold_in(rng, 2), number_of)]


def scatter_about(own_key, dims, deviation, bound, cuts=(), kind=jnp.bfloat16):
    gain = block_scale(own_key, dims, cuts, -0.22, 0.18) if cuts else 1.0
    result = jax.random.normal(own_key, dims, jnp.float32) * deviation * gain
    return jnp.minimum(jnp.maximum(result, -bound), bound).astype(kind)


def gaussian_with(stream_key, shape, deviation, most, shards, heavy, kind=jnp.bfloat16):
    result = deviation * jax.random.normal(stream_key, shape, jnp.float32)
    if shards:
        result = result * block_scale(stream_key, shape, shards, -0.22, 0.18)
    return jnp.clip(strengthened(result, jax.random.fold_in(stream_key, 3), *heavy), -most, most).astype(kind)


def setup_inputs(seed: int = 0) -> dict:
    seeds = jax.random.split(jax.random.key(seed), 17)
    return {
        "hidden_act": gaussian_with(seeds[0], (TOKENS, EW, FF), 1.0, 12.0, ((0, 32),), (0, 2, 32, 2.75)),
        "out_grad": scatter_about(seeds[1], (TOKENS, EW, D), ((TOK_DEV * N_DP) ** -0.5), 0.03125, ((0, 32), (2, 8))),
        "router_grads": gaussian_with(seeds[2], (N_DP, EW, D), (2.0 * N_DP ** -0.5), 4.0, ((0, 32),), (0, 2, 32, 2.75), jnp.float32),
        "small_grads": gaussian_with(seeds[3], (N_DP, SMALL), (N_DP ** -0.5), 2.0, ((0, 32),), (0, 1, 32, 2.75), jnp.float32),
        "expert_ids": draw_expert_ids(jax.random.fold_in(seeds[16], 71), 0),
        "small_lengths": uneven(seeds[5], NT, SMALL, SMALL // 4, 2).astype(jnp.int32),
        "small_rate": jnp.clip(jnp.exp(jax.random.uniform(seeds[6], (NT,), jnp.float32, math.log(0.25), math.log(4.0))), 0.25, 4.0),
        "expert_w": scatter_about(seeds[7], (EW, FF, D), 1.0, 6.0, ((1, 32), (2, 8)), jnp.float32),
        "expert_m": scatter_about(seeds[8], (EW, FF, D), 0.5, 3.0, ((1, 32), (2, 8)), jnp.float32),
        "expert_v": jnp.clip(jnp.exp(math.log(4.0) - 3.6888794 * jax.random.uniform(seeds[9], (EW, FF, D), jnp.float32) ** block_scale(seeds[9], (EW, FF, D), ((1, 32), (2, 8)), -0.2, 0.2)), 0.1, 4.0),
        "router_w": scatter_about(seeds[10], (NE, D), 1.0, 6.0, ((1, 32),), jnp.float32),
        "router_m": scatter_about(seeds[11], (NE, D), 0.5, 3.0, ((1, 32),), jnp.float32),
        "router_v": jnp.clip(jnp.exp(math.log(4.0) - 3.6888794 * jax.random.uniform(seeds[12], (NE, D), jnp.float32) ** block_scale(seeds[12], (NE, D), ((1, 32),), -0.2, 0.2)), 0.1, 4.0),
        "small_w": jnp.clip(1.0 + 0.1 * jax.random.normal(seeds[13], (SMALL,), jnp.float32), 0.5, 1.5),
        "small_m": scatter_about(seeds[14], (SMALL,), 0.5, 3.0, ((0, 32),), jnp.float32),
        "small_v": jnp.clip(jnp.exp(math.log(4.0) - 3.6888794 * jax.random.uniform(seeds[15], (SMALL,), jnp.float32) ** block_scale(seeds[15], (SMALL,), ((0, 32),), -0.2, 0.2)), 0.1, 4.0),
    }


beta_one = 0.9
beta_two = 0.95
learn_rate = 0.1
decay_rate = 0.1
eps = 1e-08
adam_step = 12

def adamw(weight, moment, second, grad, factor, decay):
    moment_new = beta_one * moment + (1.0 - beta_one) * grad
    second_new = beta_two * second + (1.0 - beta_two) * grad * grad
    corrected = moment_new / (1.0 - beta_one ** adam_step)
    scaled = second_new / (1.0 - beta_two ** adam_step)
    weight_new = weight - learn_rate * factor * (corrected / (jnp.sqrt(scaled) + eps) + decay * weight)
    return (weight_new, moment_new, second_new)

def reference(hidden_act, out_grad, router_grads, small_grads, expert_ids, small_lengths, small_rate, expert_w, expert_m, expert_v, router_w, router_m, router_v, small_w, small_m, small_v):
    expert_grad = jnp.stack([jnp.dot(hidden_act[:, e, :].T, out_grad[:, e, :], preferred_element_type=jnp.float32) for e in range(EW)])
    router_sum = lax.optimization_barrier(jnp.sum(router_grads, axis=0))
    router_grad = jnp.zeros((NE, D), jnp.float32).at[expert_ids].add(router_sum)
    small_grad = lax.optimization_barrier(jnp.sum(small_grads, axis=0))
    ends = jnp.cumsum(small_lengths).astype(jnp.int32)
    places = jnp.arange(SMALL, dtype=jnp.int32)
    tensor_of = lax.optimization_barrier(jnp.sum((places[:, None] >= ends[None, :]).astype(jnp.int32), axis=1))
    small_factor = small_rate[tensor_of]
    new_expert, expert_moment, expert_second = adamw(expert_w, expert_m, expert_v, expert_grad, 1.0, decay_rate)
    new_router, router_moment, router_second = adamw(router_w, router_m, router_v, router_grad, 1.0, decay_rate)
    new_small, small_moment, small_second = adamw(small_w, small_m, small_v, small_grad, small_factor, 0.0)
    return (new_expert, expert_moment, expert_second, new_router, router_moment, router_second, new_small, small_moment, small_second, new_expert.astype(jnp.bfloat16), new_router.astype(jnp.bfloat16), new_small.astype(jnp.bfloat16))
```

```python
import jax
import jax.numpy as jnp
from jax import lax
from jax.sharding import Mesh, PartitionSpec as P

beta_one = 0.9
beta_two = 0.95
learn_rate = 0.1
decay_rate = 0.1
eps = 1e-08
adam_step = 12

AXES = ("x", "zl", "core", "y", "zh")
SIZES = (4, 4, 2, 4, 2)
DP = AXES[:3]
GROUP = AXES[3:]
NX, NZ, NC, NY, NH = SIZES


def adamw(weight, moment, second, grad, factor, decay):
    moment_new = beta_one * moment + (1.0 - beta_one) * grad
    second_new = beta_two * second + (1.0 - beta_two) * grad * grad
    corrected = moment_new / (1.0 - beta_one**adam_step)
    scaled = second_new / (1.0 - beta_two**adam_step)
    weight_new = weight - learn_rate * factor * (
        corrected / (jnp.sqrt(scaled) + eps) + decay * weight
    )
    return (weight_new, moment_new, second_new)


def shift(value, axis, size, step):
    return lax.ppermute(value, axis, [(i, (i + step) % size) for i in range(size)])


def swap_core(value):
    return lax.ppermute(value, "core", [(0, 1), (1, 0)])


def flat(x, zl, core, y, zh):
    return (((x * NZ + zl) * NC + core) * NY + y) * NH + zh


def to_owner_group():
    pairs = []
    for x in range(NX):
        for zl in range(NZ):
            a, b = zl // 2, zl % 2
            for core in range(NC):
                for y in range(NY):
                    for zh in range(NH):
                        pairs.append((flat(x, zl, core, y, zh), flat(y, 2 * zh + b, core, x, a)))
    return pairs


def pick(value, index, axis):
    return lax.dynamic_index_in_dim(value, index, axis, keepdims=False)


def expert_reduce(hidden_act, out_grad, ix, iz, ic):
    experts, hidden, feats = hidden_act.shape[1], hidden_act.shape[2], out_grad.shape[2]
    wide = hidden // NX
    rows = wide // (NZ * NC)
    total = None
    arrived = []
    for k in (2, 1, 3, 0):
        part = lax.dynamic_slice_in_dim(hidden_act, ((ix + k) % NX) * wide, wide, 2)
        grad = jnp.einsum("tef,ted->efd", part, out_grad, preferred_element_type=jnp.float32)
        grad = grad.astype(jnp.bfloat16).reshape(experts, NZ, NC, rows, feats)
        theirs = swap_core(pick(grad, 1 - ic, 2))
        both = pick(grad, ic, 2).astype(jnp.float32) + theirs.astype(jnp.float32)
        if k:
            arrived.append(shift(both.astype(jnp.bfloat16), "x", NX, k))
        else:
            total = both
    for other in arrived:
        total = total + other.astype(jnp.float32)
    low = total.astype(jnp.bfloat16)
    result = pick(total, iz, 1)
    for j in (1, 2, 3):
        result = result + shift(pick(low, (iz + j) % NZ, 1), "zl", NZ, j).astype(jnp.float32)
    return result


def body(
    hidden_act,
    out_grad,
    router_grads,
    small_grads,
    expert_ids,
    small_lengths,
    small_rate,
    expert_w,
    expert_m,
    expert_v,
    router_w,
    router_m,
    router_v,
    small_w,
    small_m,
    small_v,
):
    ix, iz, ic = lax.axis_index("x"), lax.axis_index("zl"), lax.axis_index("core")
    dp_index = (ix * NZ + iz) * NC + ic
    n_dp = NX * NZ * NC

    selected = router_grads.shape[1]
    router_cols = router_w.shape[1]
    shard_len = small_w.shape[0]
    packed = jnp.concatenate(
        [
            router_grads[0].reshape(selected, n_dp, router_cols).swapaxes(0, 1).reshape(n_dp, -1),
            small_grads[0].reshape(n_dp, shard_len),
        ],
        axis=1,
    ).astype(jnp.bfloat16)
    packed = lax.all_to_all(packed, DP, 0, 0, tiled=True)
    packed = jnp.sum(packed.astype(jnp.float32), axis=0)
    router_part = packed[: selected * router_cols].reshape(selected, router_cols)
    small_part = packed[selected * router_cols :]

    experts_all = router_w.shape[0]
    selector = (expert_ids[:, None] == jnp.arange(experts_all, dtype=jnp.int32)[None, :]).astype(
        jnp.float32
    )
    router_grad = jnp.sum(selector[:, :, None] * router_part[:, None, :], axis=0)
    new_router, router_moment, router_second = adamw(
        router_w, router_m, router_v, router_grad, 1.0, decay_rate
    )
    places = dp_index * shard_len + jnp.arange(shard_len, dtype=jnp.int32)
    ends = jnp.cumsum(small_lengths)
    tensor_of = jnp.sum((places[:, None] >= ends[None, :]).astype(jnp.int32), axis=1)
    tensor_count = small_rate.shape[0]
    picked = (tensor_of[:, None] == jnp.arange(tensor_count, dtype=jnp.int32)[None, :]).astype(
        jnp.float32
    )
    small_factor = jnp.sum(picked * small_rate[None, :], axis=1)
    new_small, small_moment, small_second = adamw(
        small_w, small_m, small_v, small_part, small_factor, 0.0
    )

    extra = 16
    mine = jnp.concatenate(
        [
            new_router.astype(jnp.bfloat16),
            jnp.pad(
                new_small.astype(jnp.bfloat16).reshape(-1, router_cols),
                ((0, extra - shard_len // router_cols), (0, 0)),
            ),
        ],
        axis=0,
    )
    height = experts_all + extra
    line = jnp.zeros((height, NZ, router_cols), jnp.bfloat16)
    for j in range(NZ):
        piece = mine if j == 0 else shift(mine, "zl", NZ, j)
        line = lax.dynamic_update_slice(line, piece[:, None], (0, (iz - j) % NZ, 0))
    plane = jnp.zeros((height, NX, NZ, NC, router_cols), jnp.bfloat16)
    for k in range(NX):
        piece = line if k == 0 else shift(line, "x", NX, k)
        for core, block in ((ic, piece), (1 - ic, swap_core(piece))):
            plane = lax.dynamic_update_slice(
                plane, block[:, None, :, None], (0, (ix - k) % NX, 0, core, 0)
            )
    router_rollout = plane[:experts_all].reshape(experts_all, -1)
    small_rollout = (
        plane[experts_all : experts_all + shard_len // router_cols]
        .reshape(shard_len // router_cols, n_dp, router_cols)
        .swapaxes(0, 1)
        .reshape(-1)
    )

    expert_grad = expert_reduce(hidden_act, out_grad, ix, iz, ic)
    new_expert, expert_moment, expert_second = adamw(
        expert_w, expert_m, expert_v, expert_grad, 1.0, decay_rate
    )
    experts, rows, feats = expert_w.shape
    low = lax.ppermute(new_expert.astype(jnp.bfloat16), AXES, to_owner_group())
    half = jnp.zeros((experts, 2, rows, NH, feats), jnp.bfloat16)
    for j in range(NZ):
        piece = low if j == 0 else shift(low, "zl", NZ, j)
        came = (iz - j) % NZ
        half = lax.dynamic_update_slice(
            half, piece[:, None, :, None], (0, came % 2, 0, came // 2, 0)
        )
    half = half.reshape(experts, 2, rows, NH * feats)
    whole = jnp.zeros((experts, 2, NC, rows, NY * NH * feats), jnp.bfloat16)
    for k in range(NX):
        piece = half if k == 0 else shift(half, "x", NX, k)
        at = ((ix - k) % NX) * (NH * feats)
        for core, block in ((ic, piece), (1 - ic, swap_core(piece))):
            whole = lax.dynamic_update_slice(whole, block[:, :, None], (0, 0, core, 0, at))
    expert_rollout = whole.reshape(experts, 2 * NC * rows, NY * NH * feats)
    return (
        new_expert,
        expert_moment,
        expert_second,
        new_router,
        router_moment,
        router_second,
        new_small,
        small_moment,
        small_second,
        expert_rollout,
        router_rollout,
        small_rollout,
    )


def solution(mesh):
    fine = Mesh(mesh.devices.reshape(SIZES), AXES)
    placed = (
        P(DP, None, None),
        P(DP, None, GROUP),
        P(DP, None, None),
        P(DP, None),
        P(),
        P(),
        P(),
        P(None, DP, GROUP),
        P(None, DP, GROUP),
        P(None, DP, GROUP),
        P(None, DP),
        P(None, DP),
        P(None, DP),
        P(DP),
        P(DP),
        P(DP),
    )
    return jax.shard_map(
        body,
        mesh=fine,
        in_specs=placed,
        out_specs=(
            P(None, DP, GROUP),
            P(None, DP, GROUP),
            P(None, DP, GROUP),
            P(None, DP),
            P(None, DP),
            P(None, DP),
            P(DP),
            P(DP),
            P(DP),
            P(None, GROUP, None),
            P(),
            P(),
        ),
        check_vma=False,
    )
```

```python
import jax
import jax.numpy as jnp
from jax import lax
from jax.experimental import pallas as pl
from jax.experimental.pallas import tpu as pltpu
from jax.sharding import Mesh, PartitionSpec as P

beta_one = 0.9
beta_two = 0.95
learn_rate = 0.1
decay_rate = 0.1
eps = 1e-08
adam_step = 12

AXES = ("x", "zl", "core", "y", "zh")
SIZES = (4, 4, 2, 4, 2)
DP = AXES[:3]
GROUP = AXES[3:]
NX, NZ, NC, NY, NH = SIZES
EXTRA = 16

SCALARS = pl.BlockSpec(memory_space=pltpu.SMEM)
LOCAL = pl.BlockSpec(memory_space=pltpu.VMEM)
FAR = pl.BlockSpec(memory_space=pltpu.HBM)


def adamw(weight, moment, second, grad, factor, decay):
    moment_new = beta_one * moment + (1.0 - beta_one) * grad
    second_new = beta_two * second + (1.0 - beta_two) * grad * grad
    corrected = moment_new / (1.0 - beta_one**adam_step)
    scaled = second_new / (1.0 - beta_two**adam_step)
    weight_new = weight - learn_rate * factor * (
        corrected / (jnp.sqrt(scaled) + eps) + decay * weight
    )
    return (weight_new, moment_new, second_new)


def shift(value, axis, size, step):
    return lax.ppermute(value, axis, [(i, (i + step) % size) for i in range(size)])


def swap_core(value):
    return lax.ppermute(value, "core", [(0, 1), (1, 0)])


def flat(x, zl, core, y, zh):
    return (((x * NZ + zl) * NC + core) * NY + y) * NH + zh


def to_owner_group():
    pairs = []
    for x in range(NX):
        for zl in range(NZ):
            a, b = zl // 2, zl % 2
            for core in range(NC):
                for y in range(NY):
                    for zh in range(NH):
                        to = flat((x + y) % NX, 2 * zh + b, core, x, a)
                        pairs.append((flat(x, zl, core, y, zh), to))
    return pairs


def to_float(value):
    return value.astype(jnp.float32)


def to_low(value):
    return value.astype(jnp.bfloat16)


def numbers(*values):
    return jnp.stack([jnp.asarray(v, jnp.int32) for v in values])


def kernel(body, outs, ins, out_specs=None, scratch=(), aliases=None, name=None, room=12):
    shapes = [jax.ShapeDtypeStruct(*o) for o in outs]
    return pl.pallas_call(
        body,
        out_shape=shapes,
        in_specs=ins,
        out_specs=out_specs or [LOCAL] * len(outs),
        scratch_shapes=list(scratch),
        input_output_aliases=aliases or {},
        cost_estimate=pl.CostEstimate(flops=0, bytes_accessed=0, transcendentals=0),
        compiler_params=pltpu.CompilerParams(vmem_limit_bytes=room * 2**20),
        name=name,
    )


def fetch(sources, targets, sems):
    copies = [
        pltpu.make_async_copy(a, b, sems.at[n]) for n, (a, b) in enumerate(zip(sources, targets))
    ]
    for copy in copies:
        copy.start()
    return copies


def take_kernel(place, source, *refs):
    *outs, sems = refs
    parts = 8
    copies = []
    for n, out in enumerate(outs):
        tokens, _, wide = out.shape
        at = pl.multiple_of(place[n] * wide, 128)
        for p in range(parts):
            rows = pl.ds(p * (tokens // parts), tokens // parts)
            copies.append(
                pltpu.make_async_copy(
                    source.at[rows, :, pl.ds(at, wide)], out.at[rows], sems.at[len(copies)]
                )
            )
            copies[-1].start()
    for copy in copies:
        copy.wait()


def take(hidden_act, indices, room):
    tokens, experts, hidden = hidden_act.shape
    call = kernel(
        take_kernel,
        [((tokens, experts, hidden // NX), hidden_act.dtype)] * len(indices),
        [SCALARS, FAR],
        scratch=[pltpu.SemaphoreType.DMA((8 * len(indices),))],
        name="take",
        room=room,
    )
    return call(numbers(*indices), hidden_act)


def hold_kernel(*refs):
    *refs, sems = refs
    far, near = refs[: len(refs) // 2], refs[len(refs) // 2 :]
    for copy in fetch(far, near, sems):
        copy.wait()


def hold(*values):
    call = kernel(
        hold_kernel,
        [(v.shape, v.dtype) for v in values],
        [FAR] * len(values),
        scratch=[pltpu.SemaphoreType.DMA((len(values),))],
        name="hold",
    )
    return call(*values)


def extras_kernel(router, small, out, wide):
    cols, shard = 128, 256
    wide[...] = jnp.zeros_like(wide)
    for x in range(NX):
        for d in range(NZ * NC):
            at = x * NZ * NC + d
            for e in range(2):
                wide[x, d : d + 1, e * cols : (e + 1) * cols] = router[
                    e : e + 1, at * cols : (at + 1) * cols
                ]
            wide[x, d : d + 1, 2 * cols : 2 * cols + shard] = small[
                0:1, at * shard : (at + 1) * shard
            ]
    out[...] = to_low(wide[...])


def pack_extras(router_grads, small_grads):
    feats = 512
    call = kernel(
        extras_kernel,
        [((NX, EXTRA, feats), jnp.bfloat16)],
        [LOCAL, LOCAL],
        scratch=[pltpu.VMEM((NX, EXTRA, feats), jnp.float32)],
        name="extras",
    )
    return call(router_grads, small_grads)[0]


def both_cores(place, own, theirs, e, zl):
    rows = own.shape[1] // (NZ * NC)
    at = pl.multiple_of((zl * NC + place[0]) * rows, 16)
    return to_float(own[e, pl.ds(at, rows), :]) + to_float(theirs[e, pl.ds(at, rows), :])


def far_kernel(place, own, theirs, extras, up, down):
    experts, wide, feats = own.shape
    rows = wide // (NZ * NC)
    for e, out in enumerate((up, down)):
        for zl in range(NZ):
            out[zl * rows : (zl + 1) * rows, :] = to_low(both_cores(place, own, theirs, e, zl))
    up[NZ * rows :, :] = extras[place[1]]


def pair_far(place, own, theirs, extras):
    experts, wide, feats = own.shape
    rows = wide // NC
    call = kernel(
        far_kernel,
        [((rows + EXTRA, feats), jnp.bfloat16), ((rows, feats), jnp.bfloat16)],
        [SCALARS] + [LOCAL] * 3,
        name="pair_far",
    )
    return call(place, own, theirs, extras)


def near_kernel(place, own_up, theirs_up, own_down, theirs_down, extras, up, down, to_up, to_down):
    experts, wide, feats = own_up.shape
    rows = wide // (NZ * NC)
    half = NZ * rows
    for n, (own, theirs, out) in enumerate(
        ((own_up, theirs_up, to_up), (own_down, theirs_down, to_down))
    ):
        for e in range(experts):
            for zl in range(NZ):
                total = both_cores(place, own, theirs, e, zl)
                if e == n:
                    more = (up, down)[n]
                    total = total + to_float(more[zl * rows : (zl + 1) * rows, :])
                at = (e * NZ + zl) * rows
                out[at : at + rows, :] = to_low(total)
    to_up[2 * half :, :] = to_low(to_float(extras[place[1]]) + to_float(up[half:, :]))
    to_down[2 * half :, :] = extras[place[2]]


def pair_near(place, ups, downs, extras, up, down):
    experts, wide, feats = ups[0].shape
    rows = experts * wide // NC + EXTRA
    call = kernel(
        near_kernel,
        [((rows, feats), jnp.bfloat16)] * 2,
        [SCALARS] + [LOCAL] * 7,
        name="pair_near",
    )
    return call(place, *ups, *downs, extras, up, down)


def total_kernel(place, own, theirs, extras, r1, r2, mine, s1, s2, s3):
    experts, wide, feats = own.shape
    rows = wide // (NZ * NC)
    count = experts * NZ * rows
    more = to_float(extras[place[1]]) + to_float(r1[count:, :]) + to_float(r2[count:, :])
    for j, out in enumerate((mine, s1, s2, s3)):
        zl = lax.rem(place[2] + j, NZ)
        for e in range(experts):
            total = both_cores(place, own, theirs, e, zl)
            at = pl.multiple_of((e * NZ + zl) * rows, 16)
            for r in (r1, r2):
                total = total + to_float(r[pl.ds(at, rows), :])
            out[e * rows : (e + 1) * rows, :] = total.astype(out.dtype)
        out[experts * rows :, :] = more.astype(out.dtype)


def total_up(place, own, theirs, extras, arrived):
    experts, wide, feats = own.shape
    rows = experts * wide // (NC * NZ) + EXTRA
    call = kernel(
        total_kernel,
        [((rows, feats), jnp.float32)] + [((rows, feats), jnp.bfloat16)] * 3,
        [SCALARS] + [LOCAL] * 5,
        name="total",
    )
    return call(place, own, theirs, extras, *arrived)


def expert_kernel(mine, r1, r2, r3, w, m, v, new, moment, second, low, more):
    experts, rows, feats = w.shape
    at = slice(experts * rows, experts * rows + EXTRA)
    more[...] = mine[at, :] + to_float(r1[at, :]) + to_float(r2[at, :]) + to_float(r3[at, :])
    for e in range(experts):
        at = slice(e * rows, (e + 1) * rows)
        grad = mine[at, :] + to_float(r1[at, :]) + to_float(r2[at, :]) + to_float(r3[at, :])
        weight, first, squared = adamw(w[e], m[e], v[e], grad, 1.0, decay_rate)
        new[e] = weight
        moment[e] = first
        second[e] = squared
        low[e] = to_low(weight)


def expert_update(mine, arrived, w, m, v):
    state = (w.shape, jnp.float32)
    call = kernel(
        expert_kernel,
        [state, state, state, (w.shape, jnp.bfloat16), ((EXTRA, w.shape[2]), jnp.float32)],
        [LOCAL] * 7,
        name="expert_update",
    )
    return call(mine, *arrived, w, m, v)


def others_kernel(place, ids, lengths, rate, own, theirs, *refs):
    w, m, v, sw, sm, sv = refs[:6]
    new, moment, second, small_new, small_moment, small_second, low, held = refs[6:]
    tall, cols = w.shape
    shard_rows = sw.shape[0]
    rows = lax.broadcasted_iota(jnp.int32, own.shape, 0)
    grad_row = jnp.sum(
        jnp.where(rows == place[0], own[...] + theirs[...], 0.0), axis=0, keepdims=True
    )
    at = lax.broadcasted_iota(jnp.int32, (tall, cols), 0)
    grad = jnp.zeros((tall, cols), jnp.float32)
    for e in range(ids.shape[0]):
        part = grad_row[:, e * cols : (e + 1) * cols]
        grad = grad + jnp.where(at == ids[e], part, 0.0)
    held[...] = jnp.zeros_like(held)
    for i in range(shard_rows):
        part = (ids.shape[0] + i) * cols
        held[i : i + 1, :cols] = grad_row[:, part : part + cols]
    small_grad = held[:shard_rows, :cols]
    held[...] = jnp.zeros_like(held)
    spot = (
        place[2]
        + lax.broadcasted_iota(jnp.int32, (shard_rows, cols), 0) * cols
        + lax.broadcasted_iota(jnp.int32, (shard_rows, cols), 1)
    )
    factor = jnp.zeros((shard_rows, cols), jnp.float32)
    begin = jnp.int32(0)
    for k in range(lengths.shape[0]):
        end = begin + lengths[k]
        factor = jnp.where((spot >= begin) & (spot < end), rate[k], factor)
        begin = end
    weight, first, squared = adamw(w[...], m[...], v[...], grad, 1.0, decay_rate)
    new[...] = weight
    moment[...] = first
    second[...] = squared
    rows = lax.broadcasted_iota(jnp.int32, (held.shape[0], cols), 0)
    for e in range(ids.shape[0]):
        picked = jnp.sum(jnp.where(at == ids[e], weight, 0.0), axis=0, keepdims=True)
        held[:, e * cols : (e + 1) * cols] = jnp.where(rows == place[1], picked, 0.0)
    weight, first, squared = adamw(sw[...], sm[...], sv[...], small_grad, factor, 0.0)
    small_new[...] = weight
    small_moment[...] = first
    small_second[...] = squared
    for i in range(shard_rows):
        part = (ids.shape[0] + i) * cols
        held[:, part : part + cols] = jnp.where(rows == place[1], weight[i : i + 1, :], 0.0)
    low[...] = to_low(held[...])


def others_update(place, ids, lengths, rate, own, theirs, router, small):
    tall, cols = router[0].shape
    state, packed = (router[0].shape, jnp.float32), (small[0].shape, jnp.float32)
    call = kernel(
        others_kernel,
        [state] * 3 + [packed] * 3 + [(own.shape, jnp.bfloat16)],
        [SCALARS] * 4 + [LOCAL] * 8,
        scratch=[pltpu.VMEM(own.shape, jnp.float32)],
        name="others_update",
    )
    return call(place, ids, lengths, rate, own, theirs, *router, *small)


def join_kernel(low, extras, out):
    experts, rows, feats = low.shape
    for e in range(experts):
        out[e * rows : (e + 1) * rows, :] = low[e]
    out[experts * rows :, :] = extras[...]


def join(low, extras):
    experts, rows, feats = low.shape
    shape = (experts * rows + EXTRA, feats)
    return kernel(join_kernel, [(shape, jnp.bfloat16)], [LOCAL] * 2, name="join")(low, extras)[0]


def halve_kernel(place, *refs):
    *pieces, upper, lower = refs
    tall, feats = pieces[0].shape
    rows = (tall - EXTRA) // 2
    for s in range(NZ):
        for j in range(NZ):

            @pl.when(lax.rem(place[0] - j + NZ, NZ) == s)
            def _():
                for e, out in enumerate((upper, lower)):
                    to = (s % 2) * rows
                    out[to : to + rows, (s // 2) * feats : (s // 2 + 1) * feats] = pieces[j][
                        e * rows : (e + 1) * rows, :
                    ]

    extras = to_float(pieces[0][2 * rows :, :])
    for piece in pieces[1:]:
        extras = extras + to_float(piece[2 * rows :, :])
    upper[2 * rows :, :feats] = to_low(extras)
    upper[2 * rows :, feats:] = jnp.zeros((EXTRA, feats), jnp.bfloat16)


def halve(place, pieces):
    tall, feats = pieces[0].shape
    rows = tall - EXTRA
    call = kernel(
        halve_kernel,
        [((rows + EXTRA, NH * feats), jnp.bfloat16), ((rows, NH * feats), jnp.bfloat16)],
        [SCALARS] + [LOCAL] * NZ,
        name="halve",
    )
    return call(place, *pieces)


def finish_kernel(place, ids, router, *refs):
    pieces, refs = refs[:16], refs[16:]
    out, patched, small = refs[:3]
    near, refs = refs[3:19], refs[19:]
    lines, packed, sems, out_sems = refs
    cols = 128
    rows = out.shape[3]
    wide = near[0].shape[1]
    feats = wide // NH
    arriving = fetch(pieces, near, sems)
    leaving = []
    for n, piece in enumerate(near):
        core = place[0] ^ (n % 2)
        e = n // 2 % 2
        at = pl.multiple_of(place[1 + n // 4] * wide, wide)
        arriving[n].wait()
        for b in range(2):
            leaving.append(
                pltpu.make_async_copy(
                    piece.at[b * rows : (b + 1) * rows, :],
                    out.at[e, b, core, :, pl.ds(at, wide)],
                    out_sems.at[len(leaving)],
                )
            )
            leaving[-1].start()
    for n in range(2):
        core = place[0] ^ n
        extras = sum(to_float(p[2 * rows :, :feats]) for p in near[n::4])
        for r in range(NX * NZ):
            d = r * NC + core
            for e in range(2):
                lines[e : e + 1, pl.ds(pl.multiple_of(d * cols, cols), cols)] = extras[
                    r : r + 1, e * cols : (e + 1) * cols
                ]
            for i in range(2):
                part = (2 + i) * cols
                packed[pl.ds(2 * d + i, 1), :] = extras[r : r + 1, part : part + cols]
    small[...] = to_low(packed[...])
    spot = lax.broadcasted_iota(jnp.int32, (16, router.shape[1]), 0)
    for at in range(0, router.shape[0], 16):
        block = router[at : at + 16, :]
        patched[at : at + 16, :] = block

        @pl.when((ids[0] // 16 == at // 16) | (ids[1] // 16 == at // 16))
        def _():
            value = to_float(block)
            for e in range(2):
                value = jnp.where(spot + at == ids[e], lines[e : e + 1, :], value)
            patched[at : at + 16, :] = to_low(value)

    for copy in leaving:
        copy.wait()


def finish(place, ids, router, pieces):
    n_dp = NX * NZ * NC
    rows, wide = pieces[2].shape
    shape = (2, 2, NC, rows // 2, NY * wide)
    call = kernel(
        finish_kernel,
        [
            (shape, jnp.bfloat16),
            (router.shape, jnp.bfloat16),
            ((2 * n_dp, 128), jnp.bfloat16),
        ],
        [SCALARS] * 2 + [LOCAL] + [FAR] * len(pieces),
        out_specs=[FAR, LOCAL, LOCAL],
        scratch=[pltpu.VMEM(p.shape, jnp.bfloat16) for p in pieces]
        + [
            pltpu.VMEM((2, router.shape[1]), jnp.float32),
            pltpu.VMEM((2 * n_dp, 128), jnp.float32),
            pltpu.SemaphoreType.DMA((len(pieces),)),
            pltpu.SemaphoreType.DMA((2 * len(pieces),)),
        ],
        name="finish",
    )
    return call(place, ids, router, *pieces)


def body(
    hidden_act,
    out_grad,
    router_grads,
    small_grads,
    expert_ids,
    small_lengths,
    small_rate,
    expert_w,
    expert_m,
    expert_v,
    router_w,
    router_m,
    router_v,
    small_w,
    small_m,
    small_v,
):
    ix, iy, iz, ic = (lax.axis_index(name) for name in ("x", "y", "zl", "core"))
    dp_index = (ix * NZ + iz) * NC + ic
    shard_len = small_w.shape[0]

    router_rollout = lax.all_gather(
        to_low(adamw(router_w, router_m, router_v, jnp.zeros_like(router_w), 1.0, decay_rate)[0]),
        DP,
        axis=1,
        tiled=True,
    )

    def product(part):
        grad = jnp.einsum("tef,ted->efd", part, out_grad, preferred_element_type=jnp.float32)
        return to_low(grad), swap_core(to_low(grad))

    extras = pack_extras(router_grads[0], small_grads)
    opposite, above, below = ((ix + k) % NX for k in (2, 1, 3))
    far_away = product(take(hidden_act, [opposite], 57)[0])
    parts = take(hidden_act, [above, below, ix], 12)
    ups, downs, own = (product(part) for part in parts)
    up, down = pair_far(numbers(ic, opposite), *far_away, extras)
    up, down = shift(up, "x", NX, 1), shift(down, "x", NX, 3)
    up, down = pair_near(numbers(ic, above, below), ups, downs, extras, up, down)
    arrived = [shift(up, "x", NX, 1), shift(down, "x", NX, 3)]
    mine, *sends = total_up(numbers(ic, ix, iz), *own, extras, arrived)
    arrived = [shift(send, "zl", NZ, j + 1) for j, send in enumerate(sends)]

    small_state = [s.reshape(-1, 128) for s in (small_w, small_m, small_v)]
    state = hold(expert_w, expert_m, expert_v, router_w, router_m, router_v, *small_state)
    new_expert, expert_moment, expert_second, low, more = expert_update(
        mine, arrived, *state[:3]
    )
    others = others_update(
        numbers(iz * NC + ic, ix * NZ + iz, dp_index * shard_len),
        expert_ids,
        small_lengths,
        small_rate,
        more,
        swap_core(more),
        state[3:6],
        state[6:],
    )
    new_router, router_moment, router_second = others[:3]
    new_small, small_moment, small_second = (s.reshape(-1) for s in others[3:6])

    low = join(lax.ppermute(low, AXES, to_owner_group()), others[6])
    upper, lower = halve(numbers(iz), [low] + [shift(low, "zl", NZ, j) for j in (1, 2, 3)])
    from_below = shift(upper, "x", NX, 1), shift(lower, "x", NX, 1)
    from_above = shift(upper, "x", NX, 3), shift(lower, "x", NX, 3)
    opposite = shift(from_below[0], "x", NX, 1), shift(from_above[1], "x", NX, 3)
    pieces = []
    for piece in (upper, lower) + from_below + from_above + opposite:
        pieces += [piece, swap_core(piece)]
    places = numbers(ic, *((ix - iy - k) % NX for k in (0, 1, 3, 2)))
    whole, router_rollout, small_rollout = finish(places, expert_ids, router_rollout, pieces)
    expert_rollout = whole.reshape(whole.shape[0], -1, whole.shape[-1])
    small_rollout = small_rollout.reshape(-1)
    return (
        new_expert,
        expert_moment,
        expert_second,
        new_router,
        router_moment,
        router_second,
        new_small,
        small_moment,
        small_second,
        expert_rollout,
        router_rollout,
        small_rollout,
    )


def solution(mesh):
    fine = Mesh(mesh.devices.reshape(SIZES), AXES)
    placed = (
        P(DP, None, None),
        P(DP, None, GROUP),
        P(DP, None, None),
        P(DP, None),
        P(),
        P(),
        P(),
        P(None, DP, GROUP),
        P(None, DP, GROUP),
        P(None, DP, GROUP),
        P(None, DP),
        P(None, DP),
        P(None, DP),
        P(DP),
        P(DP),
        P(DP),
    )
    return jax.shard_map(
        body,
        mesh=fine,
        in_specs=placed,
        out_specs=(
            P(None, DP, GROUP),
            P(None, DP, GROUP),
            P(None, DP, GROUP),
            P(None, DP),
            P(None, DP),
            P(None, DP),
            P(DP),
            P(DP),
            P(DP),
            P(None, GROUP, None),
            P(),
            P(),
        ),
        check_vma=False,
    )
```

```python
import jax
import jax.numpy as jnp
from jax import lax
from jax.experimental import pallas as pl
from jax.experimental.pallas import tpu as pltpu
from jax.sharding import Mesh, PartitionSpec as P

beta_one = 0.9
beta_two = 0.95
learn_rate = 0.1
decay_rate = 0.1
eps = 1e-08
adam_step = 12

AXES = ("x", "zl", "core", "y", "zh")
SIZES = (4, 4, 2, 4, 2)
DP = AXES[:3]
GROUP = AXES[3:]
NX, NZ, NC, NY, NH = SIZES
EXTRA = 16

SCALARS = pl.BlockSpec(memory_space=pltpu.SMEM)
LOCAL = pl.BlockSpec(memory_space=pltpu.VMEM)
HELD = pl.BlockSpec(memory_space=pltpu.VMEM)
FAR = pl.BlockSpec(memory_space=pltpu.HBM)


def adamw(weight, moment, second, grad, factor, decay):
    moment_new = beta_one * moment + (1.0 - beta_one) * grad
    second_new = beta_two * second + (1.0 - beta_two) * grad * grad
    corrected = moment_new / (1.0 - beta_one**adam_step)
    scaled = second_new / (1.0 - beta_two**adam_step)
    weight_new = weight - learn_rate * factor * (
        corrected / (jnp.sqrt(scaled) + eps) + decay * weight
    )
    return (weight_new, moment_new, second_new)


def shift(value, axis, size, step):
    return lax.ppermute(value, axis, [(i, (i + step) % size) for i in range(size)])


def swap_with(value, axis, size, step):
    return lax.ppermute(value, axis, [(i, i ^ step) for i in range(size)])


def swap_core(value):
    return lax.ppermute(value, "core", [(0, 1), (1, 0)])


def flat(x, zl, core, y, zh):
    return (((x * NZ + zl) * NC + core) * NY + y) * NH + zh


def to_owner_group(step):
    pairs = []
    for x in range(NX):
        for zl in range(NZ):
            a, b = zl // 2, zl % 2
            for core in range(NC):
                for y in range(NY):
                    for zh in range(NH):
                        to = flat((x + y) % NX, (2 * zh + b) ^ step, core, x, a)
                        pairs.append((flat(x, zl, core, y, zh), to))
    return pairs


def after(value, *others):
    return lax.optimization_barrier((value,) + others)[0]


def to_float(value):
    return value.astype(jnp.float32)


def to_low(value):
    return value.astype(jnp.bfloat16)


def numbers(*values):
    return jnp.stack([jnp.asarray(v, jnp.int32) for v in values])


def kernel(body, outs, ins, scratch=(), aliases=None, name=None, cost=0, room=16):
    shapes = []
    for spec, shape, dtype in outs:
        if spec is HELD:
            shapes.append(pltpu.VMEM(shape, dtype))
        else:
            shapes.append(jax.ShapeDtypeStruct(shape, dtype))
    call = pl.pallas_call(
        body,
        out_shape=shapes,
        in_specs=ins,
        out_specs=[spec for spec, _, _ in outs],
        scratch_shapes=list(scratch),
        input_output_aliases=aliases or {},
        cost_estimate=pl.CostEstimate(flops=0, bytes_accessed=cost, transcendentals=0),
        compiler_params=pltpu.CompilerParams(vmem_limit_bytes=room * 2**20),
        name=name,
    )

    def run(*values):
        placed = []
        for spec, value in zip(ins, values):
            if spec is HELD:
                value = pltpu.with_memory_space_constraint(value, pltpu.VMEM)
            elif spec is FAR:
                value = pltpu.with_memory_space_constraint(value, pltpu.HBM)
            placed.append(value)
        return call(*placed)

    return run


def fetch(sources, targets, sems):
    copies = [
        pltpu.make_async_copy(a, b, sems.at[n]) for n, (a, b) in enumerate(zip(sources, targets))
    ]
    for copy in copies:
        copy.start()
    return copies


def product_kernel(place, hidden, grads, far_keep, far_send, keep, send, raw, left, right, sems):
    tokens, experts, wide = hidden.shape
    wide = wide // NX
    rows = wide // (NZ * NC)
    blocks = sems.shape[0]
    spans = [pl.ds(p * (tokens // blocks), tokens // blocks) for p in range(blocks)]
    copies = fetch([hidden.at[at] for at in spans], [raw.at[at] for at in spans], sems)
    for at, copy in zip(spans, copies):
        right[:, at, :] = jnp.swapaxes(grads[at], 0, 1)
        copy.wait()
        left[:, at, :] = jnp.swapaxes(raw[at], 0, 1)
    for n in range(NX):
        at = pl.multiple_of(place[1 + n] * wide, 128)
        for e in range(experts):
            value = lax.dot_general(
                left[e, :, pl.ds(at, wide)],
                right[e],
                (((0,), (0,)), ((), ())),
                preferred_element_type=jnp.float32,
            )
            mine, other = (far_keep, far_send) if n == 0 else (keep, send)
            m = max(n - 1, 0)
            for zl in range(NZ):
                first = value[2 * zl * rows : (2 * zl + 1) * rows, :]
                second = value[(2 * zl + 1) * rows : (2 * zl + 2) * rows, :]
                to = (e * NZ + zl) * rows
                mine[m, to : to + rows, :] = to_low(jnp.where(place[0] == 0, first, second))
                other[m, to : to + rows, :] = to_low(jnp.where(place[0] == 0, second, first))


def product(place, hidden_act, out_grad):
    tokens, experts, hidden = hidden_act.shape
    feats = out_grad.shape[2]
    rows = experts * hidden // NX // NC
    one, rest = (1, rows, feats), (NX - 1, rows, feats)
    call = kernel(
        product_kernel,
        [(HELD, shape, jnp.bfloat16) for shape in (one, one, rest, rest)],
        [SCALARS, FAR, LOCAL],
        scratch=[
            pltpu.VMEM(hidden_act.shape, jnp.bfloat16),
            pltpu.VMEM((experts, tokens, hidden), jnp.bfloat16),
            pltpu.VMEM((experts, tokens, feats), jnp.bfloat16),
            pltpu.SemaphoreType.DMA((4,)),
        ],
        name="product",
        room=40,
    )
    return call(place, hidden_act, out_grad)


def parts_kernel(ids, w, m, v, sw, sm, sv, out, wide):
    tall, cols = w.shape
    wide[...] = jnp.zeros_like(wide)
    at = lax.broadcasted_iota(jnp.int32, (tall, cols), 0)
    for n, (router, small) in enumerate(((w, sw), (m, sm), (v, sv))):
        values = [
            jnp.sum(jnp.where(at == ids[e], router[...], 0.0), axis=0, keepdims=True)
            for e in range(2)
        ] + [small[i : i + 1, :] for i in range(2)]
        for part, value in enumerate(values):
            lanes = slice(part * cols, (part + 1) * cols)
            top = to_float(to_low(value))
            wide[8 + 2 * n : 9 + 2 * n, lanes] = top
            wide[9 + 2 * n : 10 + 2 * n, lanes] = value - top
    out[...] = to_low(wide[...])


def selected_parts(ids, *values):
    shape = (EXTRA, 512)
    call = kernel(
        parts_kernel,
        [(HELD, shape, jnp.bfloat16)],
        [SCALARS] + [LOCAL] * len(values),
        scratch=[pltpu.VMEM(shape, jnp.float32)],
        name="parts",
        cost=2 * 2**20,
    )
    return call(ids, *values)[0]


def extras_kernel(router, small, out, wide):
    cols, shard = 128, 256
    wide[...] = jnp.zeros_like(wide)
    for x in range(NX):
        for d in range(NZ * NC):
            at = x * NZ * NC + d
            for e in range(2):
                wide[x, d : d + 1, e * cols : (e + 1) * cols] = router[
                    e : e + 1, at * cols : (at + 1) * cols
                ]
            wide[x, d : d + 1, 2 * cols : 2 * cols + shard] = small[
                0:1, at * shard : (at + 1) * shard
            ]
    out[...] = to_low(wide[...])


def pack_extras(router_grads, small_grads):
    feats = 512
    call = kernel(
        extras_kernel,
        [(LOCAL, (NX, EXTRA, feats), jnp.bfloat16)],
        [LOCAL, LOCAL],
        scratch=[pltpu.VMEM((NX, EXTRA, feats), jnp.float32)],
        name="extras",
    )
    return call(router_grads, small_grads)[0]


def both_cores(own, theirs, start, rows):
    at = pl.ds(start, rows)
    return to_float(own[at, :]) + to_float(theirs[at, :])


def far_kernel(place, own, theirs, extras, up, down):
    half = down.shape[0]
    for e, out in enumerate((up, down)):
        out[:half, :] = to_low(both_cores(own.at[0], theirs.at[0], e * half, half))
    up[half:, :] = extras[place[0]]


def pair_far(place, own, theirs, extras):
    _, rows, feats = own.shape
    call = kernel(
        far_kernel,
        [(HELD, (rows // 2 + EXTRA, feats), jnp.bfloat16), (HELD, (rows // 2, feats), jnp.bfloat16)],
        [SCALARS] + [HELD] * 3,
        name="pair_far",
    )
    return call(place, own, theirs, extras)


def near_kernel(place, own, theirs, extras, up, down, router, hop, to_up, to_down, routers):
    routers[0] = router[...]
    routers[1] = hop[...]
    half = down.shape[0]
    for n, (more, out) in enumerate(((up, to_up), (down, to_down))):
        for e in range(2):
            total = both_cores(own.at[n], theirs.at[n], e * half, half)
            if e == n:
                total = total + to_float(more[:half, :])
            out[e * half : (e + 1) * half, :] = to_low(total)
    to_up[2 * half :, :] = to_low(to_float(extras[place[0]]) + to_float(up[half:, :]))
    to_down[2 * half :, :] = extras[place[1]]


def pair_near(place, own, theirs, extras, up, down, router, hop):
    _, rows, feats = own.shape
    call = kernel(
        near_kernel,
        [(HELD, (rows + EXTRA, feats), jnp.bfloat16)] * 2
        + [(HELD, (2, *router.shape), jnp.bfloat16)],
        [SCALARS] + [HELD] * 7,
        name="pair_near",
    )
    return call(place, own, theirs, extras, up, down, router, hop)


def total_kernel(
    place, own, theirs, extras, state, r1, r2, router, hop, mine, s1, s2, s3, routers
):
    routers[:2] = router[...]
    routers[2:] = hop[...]
    _, count, feats = own.shape
    rows = count // (2 * NZ)
    more = to_float(extras[place[0]]) + to_float(r1[count:, :]) + to_float(r2[count:, :])
    more = more + to_float(state[...])
    for j, out in enumerate((mine, s1, s2, s3)):
        zl = lax.rem(place[1] + j, NZ)
        for e in range(2):
            at = pl.multiple_of((e * NZ + zl) * rows, 16)
            total = both_cores(own.at[2], theirs.at[2], at, rows)
            for r in (r1, r2):
                total = total + to_float(r[pl.ds(at, rows), :])
            out[e * rows : (e + 1) * rows, :] = total.astype(out.dtype)
        out[2 * rows :, :] = more.astype(out.dtype)


def total_up(place, own, theirs, extras, state, arrived, router, hop):
    _, count, feats = own.shape
    rows = count // NZ + EXTRA
    call = kernel(
        total_kernel,
        [(LOCAL, (rows, feats), jnp.float32)]
        + [(HELD, (rows, feats), jnp.bfloat16)] * 3
        + [(HELD, (4, *router.shape[1:]), jnp.bfloat16)],
        [SCALARS] + [HELD] * 8,
        name="total",
    )
    return call(place, own, theirs, extras, state, *arrived, router, hop)


def rate_at(spot, lengths, rate):
    factor = jnp.zeros(spot.shape, jnp.float32)
    begin = jnp.int32(0)
    for k in range(lengths.shape[0]):
        end = begin + lengths[k]
        factor = jnp.where((spot >= begin) & (spot < end), rate[k], factor)
        begin = end
    return factor


def expert_kernel(
    place, lengths, rate, r1, r2, r3, router, hop, mine_far, w_far, m_far, v_far, *refs
):
    new, moment, second, low, extras, more, routers, mine, w, m, v, sems = refs
    experts, rows, feats = w.shape
    copies = fetch((mine_far, w_far, m_far, v_far), (mine, w, m, v), sems)
    routers[:4] = router[...]
    routers[4:] = hop[...]
    copies[0].wait()

    ix, iz, ic = place[0], place[1], place[2]
    blocks = [to_float(r[experts * rows :, :]) for r in (mine, r1, r2, r3)]
    sums = blocks[0] + blocks[1] + blocks[2] + blocks[3]
    more[...] = sums
    shape = blocks[0].shape
    row = lax.broadcasted_iota(jnp.int32, shape, 0)
    lane = lax.broadcasted_iota(jnp.int32, shape, 1)
    state = [jnp.zeros(shape, jnp.float32) for _ in range(4)]
    for j, block in enumerate(blocks):
        zl = lax.rem(iz - j + NZ, NZ)
        here = row == ix * NZ + zl
        for n in range(3):
            value = block[8 + 2 * n : 9 + 2 * n, :] + block[9 + 2 * n : 10 + 2 * n, :]
            state[n] = jnp.where(here, value, state[n])
        grad = jnp.sum(jnp.where(row == zl * NC + ic, sums, 0.0), axis=0, keepdims=True)
        state[3] = jnp.where(here, grad, state[3])
    half = feats // 2
    spot = (row * NC + ic) * half + lane - half
    factor = jnp.where(lane < half, 1.0, rate_at(spot, lengths, rate))
    decay = jnp.where(lane < half, decay_rate, 0.0)
    extras[...] = to_low(adamw(*state, factor, decay)[0])

    for copy in copies[1:]:
        copy.wait()
    for e in range(experts):
        at = slice(e * rows, (e + 1) * rows)
        grad = mine[at, :] + to_float(r1[at, :]) + to_float(r2[at, :]) + to_float(r3[at, :])
        weight, first, squared = adamw(w[e], m[e], v[e], grad, 1.0, decay_rate)
        new[e] = weight
        moment[e] = first
        second[e] = squared
        low[e] = to_low(weight)


def expert_update(place, lengths, rate, mine, arrived, w, m, v, router, hop):
    state = (LOCAL, w.shape, jnp.float32)
    feats = w.shape[2]
    call = kernel(
        expert_kernel,
        [state, state, state]
        + [
            (HELD, w.shape, jnp.bfloat16),
            (HELD, (EXTRA, feats), jnp.bfloat16),
            (HELD, (EXTRA, feats), jnp.float32),
            (HELD, (8, *router.shape[1:]), jnp.bfloat16),
        ],
        [SCALARS] * 3 + [HELD] * 5 + [FAR] * 4,
        scratch=[pltpu.VMEM(mine.shape, jnp.float32)]
        + [pltpu.VMEM(w.shape, jnp.float32)] * 3
        + [pltpu.SemaphoreType.DMA((4,))],
        name="expert_update",
    )
    return call(place, lengths, rate, *arrived, router, hop, mine, w, m, v)


def others_kernel(place, ids, lengths, rate, more, w, m, v, sw, sm, sv, *refs):
    new, moment, second, small_new, small_moment, small_second, token, held = refs
    token[...] = jnp.zeros_like(token)
    tall, cols = w.shape
    shard_rows = sw.shape[0]
    rows = lax.broadcasted_iota(jnp.int32, more.shape, 0)
    grad_row = jnp.sum(jnp.where(rows == place[0], more[...], 0.0), axis=0, keepdims=True)
    at = lax.broadcasted_iota(jnp.int32, (tall, cols), 0)
    grad = jnp.zeros((tall, cols), jnp.float32)
    for e in range(ids.shape[0]):
        part = grad_row[:, e * cols : (e + 1) * cols]
        grad = grad + jnp.where(at == ids[e], part, 0.0)
    for i in range(shard_rows):
        part = (ids.shape[0] + i) * cols
        held[i : i + 1, :] = grad_row[:, part : part + cols]
    weight, first, squared = adamw(w[...], m[...], v[...], grad, 1.0, decay_rate)
    new[...] = weight
    moment[...] = first
    second[...] = squared
    spot = (
        place[1]
        + lax.broadcasted_iota(jnp.int32, (shard_rows, cols), 0) * cols
        + lax.broadcasted_iota(jnp.int32, (shard_rows, cols), 1)
    )
    factor = rate_at(spot, lengths, rate)
    weight, first, squared = adamw(
        sw[...], sm[...], sv[...], held[:shard_rows, :], factor, 0.0
    )
    small_new[...] = weight
    small_moment[...] = first
    small_second[...] = squared


def others_update(place, ids, lengths, rate, more, router, small):
    cols = router[0].shape[1]
    call = kernel(
        others_kernel,
        [(LOCAL, r.shape, jnp.float32) for r in (*router, *small)]
        + [(HELD, (8, cols), jnp.float32)],
        [SCALARS] * 4 + [HELD] + [LOCAL] * 6,
        scratch=[pltpu.VMEM((8, cols), jnp.float32)],
        name="others_update",
        cost=4 * 2**20,
    )
    return call(place, ids, lengths, rate, more, *router, *small)


def halve_kernel(place, *refs):
    pieces, (extras, token, router, hop, upper, lower, routers) = refs[:NZ], refs[NZ:]
    routers[:8] = router[...]
    routers[8:] = hop[...]
    experts, rows, feats = pieces[0].shape
    for s in range(NZ):
        for q in range(NZ):

            @pl.when((place[0] ^ q) == s)
            def _():
                for e, out in enumerate((upper, lower)):
                    to = (s % 2) * rows
                    out[to : to + rows, (s // 2) * feats : (s // 2 + 1) * feats] = pieces[q][e]

    upper[2 * rows :, :feats] = extras[...]
    upper[2 * rows :, feats:] = jnp.zeros((EXTRA, feats), jnp.bfloat16)


def halve(place, pieces, extras, token, router, hop):
    experts, rows, feats = pieces[0].shape
    call = kernel(
        halve_kernel,
        [
            (LOCAL, (2 * rows + EXTRA, NH * feats), jnp.bfloat16),
            (LOCAL, (2 * rows, NH * feats), jnp.bfloat16),
            (HELD, (16, *router.shape[1:]), jnp.bfloat16),
        ],
        [SCALARS] + [HELD] * (NZ + 4),
        name="halve",
    )
    return call(place, *pieces, extras, token, router, hop)


def lay(place, pieces, out, sems):
    rows = out.shape[3]
    copies = []
    for e, n, x, piece in pieces:
        core = place[0] ^ n
        wide = piece.shape[1]
        at = pl.multiple_of(x * wide, wide)
        for b in range(2):
            copies.append(
                pltpu.make_async_copy(
                    piece.at[b * rows : (b + 1) * rows, :],
                    out.at[e, b, core, :, pl.ds(at, wide)],
                    sems.at[len(copies)],
                )
            )
            copies[-1].start()
    return copies


def spread(core, row, d, lines, packed):
    cols = packed.shape[1]
    for e in range(2):
        at = pl.multiple_of(d * cols, cols)
        lines[e : e + 1, pl.ds(at, cols)] = row[:, e * cols : (e + 1) * cols]
    for i in range(2):
        packed[pl.ds(2 * d + i, 1), :] = row[:, (2 + i) * cols : (3 + i) * cols]


def early_kernel(place, *refs):
    far, routers, refs = refs[:12], refs[12:14], refs[14:]
    (out, patched, lines, packed), refs = refs[:4], refs[4:]
    pieces, (sems, out_sems, router_sems) = refs[:12], refs[12:]
    arriving = fetch(far, pieces, sems)
    lines[...] = jnp.zeros_like(lines)
    copies = []
    cols = packed.shape[1]
    for n, blocks in enumerate(routers):
        for z in range(NZ):
            for x in range(NX):
                d = ((place[4] ^ x) * NZ + (place[5] ^ z)) * NC + (place[0] ^ n)
                at = pl.ds(pl.multiple_of(d * cols, cols), cols)
                copies.append(
                    pltpu.make_async_copy(
                        blocks.at[z * NX + x], patched.at[:, at], router_sems.at[len(copies)]
                    )
                )
                copies[-1].start()
    for n, piece in enumerate(pieces):
        arriving[n].wait()
        spot = (n // 2 % 2, n % 2, place[1 + n // 4], piece)
        copies += lay(place, [spot], out, out_sems.at[n])
    for n in range(2):
        core = place[0] ^ n
        extras = sum(to_float(p[p.shape[0] - EXTRA :, : p.shape[1] // NH]) for p in pieces[n::4])
        for r in range(NX * NZ):
            spread(core, extras[r : r + 1, :], r * NC + core, lines, packed)
    for copy in copies:
        copy.wait()


def early(place, pieces, routers):
    rows, wide = pieces[2].shape
    n_dp = NX * NZ * NC
    tall, cols = routers[0].shape[1:]
    call = kernel(
        early_kernel,
        [
            (FAR, (2, 2, NC, rows // 2, NY * wide), jnp.bfloat16),
            (FAR, (tall, n_dp * cols), jnp.bfloat16),
            (HELD, (8, n_dp * cols), jnp.float32),
            (HELD, (2 * n_dp, cols), jnp.float32),
        ],
        [SCALARS] + [FAR] * len(pieces) + [HELD] * 2,
        scratch=[pltpu.VMEM(p.shape, p.dtype) for p in pieces]
        + [
            pltpu.SemaphoreType.DMA((len(pieces),)),
            pltpu.SemaphoreType.DMA((len(pieces), 2)),
            pltpu.SemaphoreType.DMA((n_dp,)),
        ],
        name="early",
        cost=2**20,
    )
    return call(place, *pieces, *routers)


def relay_kernel(upper, lower, lines, out):
    out[: upper.shape[0], :] = upper[...]
    out[upper.shape[0] :, :] = lower[...]


def relay(upper, lower, lines):
    shape = (upper.shape[0] + lower.shape[0], upper.shape[1])
    call = kernel(
        relay_kernel, [(HELD, shape, jnp.bfloat16)], [LOCAL, LOCAL, HELD], name="relay"
    )
    return call(upper, lower, lines)[0]


def late_kernel(place, ids, whole, router, lines, packed, own, other, *refs):
    out, patched, small, lines_now, packed_now, block, sems, block_sems = refs
    split = 2 * out.shape[3] + EXTRA
    starts = [pl.multiple_of(lax.div(ids[n], 16) * 16, 16) for n in range(2)]
    blocks = [patched.at[pl.ds(at, 16), :] for at in starts]
    arriving = fetch(blocks, [block.at[0], block.at[1]], block_sems)
    pieces = []
    for n, piece in enumerate((own, other)):
        pieces.append((0, n, place[1], piece.at[: split - EXTRA, :]))
        pieces.append((1, n, place[1], piece.at[split:, :]))
    copies = lay(place, pieces, out, sems)
    lines_now[...] = lines[...]
    packed_now[...] = packed[...]
    for n, piece in enumerate((own, other)):
        core = place[0] ^ n
        extras = to_float(piece[split - EXTRA : split, : piece.shape[1] // NH])
        at = lax.broadcasted_iota(jnp.int32, extras.shape, 0)
        for zl in range(NZ):
            r = place[2] * NZ + zl
            row = jnp.sum(jnp.where(at == r, extras, 0.0), axis=0, keepdims=True)
            spread(core, row, r * NC + core, lines_now, packed_now)
    small[...] = to_low(packed_now[...])
    spot = lax.broadcasted_iota(jnp.int32, block.shape[1:], 0)
    for copy in arriving:
        copy.wait()
    for n, at in enumerate(starts):
        value = to_float(block[n])
        for e in range(2):
            value = jnp.where(spot + at == ids[e], lines_now[e : e + 1, :], value)
        block[n] = to_low(value)
    for n in range(2):
        move = pltpu.make_async_copy(block.at[n], blocks[n], block_sems.at[n])
        move.start()
        move.wait()
    for copy in copies:
        copy.wait()


def late(place, ids, whole, router, lines, packed, own, other):
    call = kernel(
        late_kernel,
        [
            (FAR, whole.shape, jnp.bfloat16),
            (FAR, router.shape, jnp.bfloat16),
            (LOCAL, packed.shape, jnp.bfloat16),
        ],
        [SCALARS] * 2 + [FAR] * 2 + [HELD] * 4,
        scratch=[
            pltpu.VMEM(lines.shape, jnp.float32),
            pltpu.VMEM(packed.shape, jnp.float32),
            pltpu.VMEM((2, 16, router.shape[1]), jnp.bfloat16),
            pltpu.SemaphoreType.DMA((8,)),
            pltpu.SemaphoreType.DMA((2,)),
        ],
        aliases={2: 0, 3: 1},
        name="late",
    )
    return call(place, ids, whole, router, lines, packed, own, other)


def body(
    hidden_act,
    out_grad,
    router_grads,
    small_grads,
    expert_ids,
    small_lengths,
    small_rate,
    expert_w,
    expert_m,
    expert_v,
    router_w,
    router_m,
    router_v,
    small_w,
    small_m,
    small_v,
):
    ix, iy, iz, ic = (lax.axis_index(name) for name in ("x", "y", "zl", "core"))
    dp_index = (ix * NZ + iz) * NC + ic
    shard_len = small_w.shape[0]

    opposite, above, below = ((ix + k) % NX for k in (2, 1, 3))
    far_own, far_send, own, send = product(
        numbers(ic, opposite, above, below, ix), hidden_act, out_grad
    )

    zero = jnp.zeros_like(router_w)
    router = adamw(after(router_w, far_send), router_m, router_v, zero, 1.0, decay_rate)[0]
    router = to_low(router)

    extras = pack_extras(after(router_grads[0], far_send), small_grads)
    extras = to_low(to_float(extras) + to_float(swap_core(extras)))
    up, down = pair_far(numbers(opposite), far_own, swap_core(far_send), extras)
    up, down = shift(up, "x", NX, 1), shift(down, "x", NX, 3)
    theirs = swap_core(send)
    hop = swap_with(router, "x", NX, 1)
    up, down, router = pair_near(
        numbers(above, below), own, theirs, extras, up, down, router, hop
    )
    hop = swap_with(router, "x", NX, 2)
    arrived = [shift(up, "x", NX, 1), shift(down, "x", NX, 3)]
    router_state = (router_w, router_m, router_v)
    small_state = [s.reshape(-1, 128) for s in (small_w, small_m, small_v)]
    parts = selected_parts(expert_ids, *router_state, *small_state)
    mine, *sends, router = total_up(
        numbers(ix, iz), own, theirs, extras, parts, arrived, router, hop
    )
    hop = swap_with(router, "zl", NZ, 1)
    arrived = [shift(send, "zl", NZ, j + 1) for j, send in enumerate(sends)]
    new_expert, expert_moment, expert_second, low, extras, more, router = expert_update(
        numbers(ix, iz, ic),
        small_lengths,
        small_rate,
        mine,
        arrived,
        expert_w,
        expert_m,
        expert_v,
        router,
        hop,
    )
    hop = swap_with(router, "zl", NZ, 2)
    others = others_update(
        numbers(iz * NC + ic, dp_index * shard_len),
        expert_ids,
        small_lengths,
        small_rate,
        more,
        router_state,
        small_state,
    )
    new_router, router_moment, router_second = others[:3]
    new_small, small_moment, small_second = (s.reshape(-1) for s in others[3:6])

    first, second = (lax.ppermute(low, AXES, to_owner_group(q)) for q in (0, 2))
    pieces = [first, swap_with(first, "zl", NZ, 1), second, swap_with(second, "zl", NZ, 1)]
    upper, lower, router = halve(numbers(iz), pieces, extras, others[6], router, hop)
    from_below = shift(upper, "x", NX, 1), shift(lower, "x", NX, 1)
    from_above = shift(upper, "x", NX, 3), shift(lower, "x", NX, 3)
    pieces = []
    for piece in (upper, lower) + from_below + from_above:
        pieces += [piece, swap_core(piece)]
    places = [(ix - iy - k) % NX for k in (0, 1, 3, 2)]
    whole, router, lines, packed = early(
        numbers(ic, *places[:3], ix, iz), pieces, [router, swap_core(router)]
    )
    last = relay(shift(from_below[0], "x", NX, 1), shift(from_above[1], "x", NX, 3), lines)
    whole, router_rollout, small_rollout = late(
        numbers(ic, places[3], opposite),
        expert_ids,
        whole,
        router,
        lines,
        packed,
        last,
        swap_core(last),
    )
    expert_rollout = whole.reshape(whole.shape[0], -1, whole.shape[-1])
    small_rollout = small_rollout.reshape(-1)
    return (
        new_expert,
        expert_moment,
        expert_second,
        new_router,
        router_moment,
        router_second,
        new_small,
        small_moment,
        small_second,
        expert_rollout,
        router_rollout,
        small_rollout,
    )


def solution(mesh):
    fine = Mesh(mesh.devices.reshape(SIZES), AXES)
    placed = (
        P(DP, None, None),
        P(DP, None, GROUP),
        P(DP, None, None),
        P(DP, None),
        P(),
        P(),
        P(),
        P(None, DP, GROUP),
        P(None, DP, GROUP),
        P(None, DP, GROUP),
        P(None, DP),
        P(None, DP),
        P(None, DP),
        P(DP),
        P(DP),
        P(DP),
    )
    return jax.shard_map(
        body,
        mesh=fine,
        in_specs=placed,
        out_specs=(
            P(None, DP, GROUP),
            P(None, DP, GROUP),
            P(None, DP, GROUP),
            P(None, DP),
            P(None, DP),
            P(None, DP),
            P(DP),
            P(DP),
            P(DP),
            P(None, GROUP, None),
            P(),
            P(),
        ),
        check_vma=False,
    )
```

```python
import jax
import jax.numpy as jnp
from jax import lax
from jax.experimental import pallas as pl
from jax.experimental.pallas import tpu as pltpu
from jax.sharding import Mesh, PartitionSpec as P

beta_one = 0.9
beta_two = 0.95
learn_rate = 0.1
decay_rate = 0.1
eps = 1e-08
adam_step = 12

AXES = ("x", "zl", "core", "y", "zh")
SIZES = (4, 4, 2, 4, 2)
DP = AXES[:3]
GROUP = AXES[3:]
NX, NZ, NC, NY, NH = SIZES
EXTRA = 16

SCALARS = pl.BlockSpec(memory_space=pltpu.SMEM)
LOCAL = pl.BlockSpec(memory_space=pltpu.VMEM)
HELD = pl.BlockSpec(memory_space=pltpu.VMEM)
FAR = pl.BlockSpec(memory_space=pltpu.HBM)


def adamw(weight, moment, second, grad, factor, decay):
    moment_new = beta_one * moment + (1.0 - beta_one) * grad
    second_new = beta_two * second + (1.0 - beta_two) * grad * grad
    corrected = moment_new / (1.0 - beta_one**adam_step)
    scaled = second_new / (1.0 - beta_two**adam_step)
    weight_new = weight - learn_rate * factor * (
        corrected / (jnp.sqrt(scaled) + eps) + decay * weight
    )
    return (weight_new, moment_new, second_new)


def shift(value, axis, size, step):
    return lax.ppermute(value, axis, [(i, (i + step) % size) for i in range(size)])


def swap_with(value, axis, size, step):
    return lax.ppermute(value, axis, [(i, i ^ step) for i in range(size)])


def swap_core(value):
    return lax.ppermute(value, "core", [(0, 1), (1, 0)])


def flat(x, zl, core, y, zh):
    return (((x * NZ + zl) * NC + core) * NY + y) * NH + zh


def to_owner_group(step):
    pairs = []
    for x in range(NX):
        for zl in range(NZ):
            a, b = zl // 2, zl % 2
            for core in range(NC):
                for y in range(NY):
                    for zh in range(NH):
                        to = flat((x + y) % NX, (2 * zh + b) ^ step, core, x, a)
                        pairs.append((flat(x, zl, core, y, zh), to))
    return pairs


def after(value, *others):
    return lax.optimization_barrier((value,) + others)[0]


def to_float(value):
    return value.astype(jnp.float32)


def to_low(value):
    return value.astype(jnp.bfloat16)


def numbers(*values):
    return jnp.stack([jnp.asarray(v, jnp.int32) for v in values])


def kernel(body, outs, ins, scratch=(), aliases=None, name=None, cost=0, room=16):
    shapes = []
    for spec, shape, dtype in outs:
        if spec is HELD:
            shapes.append(pltpu.VMEM(shape, dtype))
        else:
            shapes.append(jax.ShapeDtypeStruct(shape, dtype))
    call = pl.pallas_call(
        body,
        out_shape=shapes,
        in_specs=ins,
        out_specs=[spec for spec, _, _ in outs],
        scratch_shapes=list(scratch),
        input_output_aliases=aliases or {},
        cost_estimate=pl.CostEstimate(flops=0, bytes_accessed=cost, transcendentals=0),
        compiler_params=pltpu.CompilerParams(vmem_limit_bytes=room * 2**20),
        name=name,
    )

    def run(*values):
        placed = []
        for spec, value in zip(ins, values):
            if spec is HELD:
                value = pltpu.with_memory_space_constraint(value, pltpu.VMEM)
            elif spec is FAR:
                value = pltpu.with_memory_space_constraint(value, pltpu.HBM)
            placed.append(value)
        return call(*placed)

    return run


def fetch(sources, targets, sems):
    copies = [
        pltpu.make_async_copy(a, b, sems.at[n]) for n, (a, b) in enumerate(zip(sources, targets))
    ]
    for copy in copies:
        copy.start()
    return copies


def product_kernel(place, hidden, grads_far, far_keep, far_send, keep, send, *scratch):
    raw, grads, left, right, sems = scratch
    tokens, experts, wide = hidden.shape
    wide = wide // NX
    rows = wide // (NZ * NC)
    blocks = sems.shape[0] - 1
    spans = [pl.ds(p * (tokens // blocks), tokens // blocks) for p in range(blocks)]
    copies = fetch(
        [grads_far] + [hidden.at[at] for at in spans], [grads] + [raw.at[at] for at in spans], sems
    )
    copies[0].wait()
    for at, copy in zip(spans, copies[1:]):
        right[:, at, :] = jnp.swapaxes(grads[at], 0, 1)
        copy.wait()
        left[:, at, :] = jnp.swapaxes(raw[at], 0, 1)
    for n in range(NX):
        at = pl.multiple_of(place[1 + n] * wide, 128)
        for e in range(experts):
            value = lax.dot_general(
                left[e, :, pl.ds(at, wide)],
                right[e],
                (((0,), (0,)), ((), ())),
                preferred_element_type=jnp.float32,
            )
            mine, other = (far_keep, far_send) if n == 0 else (keep, send)
            m = max(n - 1, 0)
            for zl in range(NZ):
                first = value[2 * zl * rows : (2 * zl + 1) * rows, :]
                second = value[(2 * zl + 1) * rows : (2 * zl + 2) * rows, :]
                to = (e * NZ + zl) * rows
                mine[m, to : to + rows, :] = to_low(jnp.where(place[0] == 0, first, second))
                other[m, to : to + rows, :] = to_low(jnp.where(place[0] == 0, second, first))


def product(place, hidden_act, out_grad):
    tokens, experts, hidden = hidden_act.shape
    feats = out_grad.shape[2]
    rows = experts * hidden // NX // NC
    one, rest = (1, rows, feats), (NX - 1, rows, feats)
    call = kernel(
        product_kernel,
        [(HELD, shape, jnp.bfloat16) for shape in (one, one, rest, rest)],
        [SCALARS, FAR, FAR],
        scratch=[
            pltpu.VMEM(hidden_act.shape, jnp.bfloat16),
            pltpu.VMEM(out_grad.shape, jnp.bfloat16),
            pltpu.VMEM((experts, tokens, hidden), jnp.bfloat16),
            pltpu.VMEM((experts, tokens, feats), jnp.bfloat16),
            pltpu.SemaphoreType.DMA((5,)),
        ],
        name="product",
        room=40,
    )
    return call(place, hidden_act, out_grad)


def parts_kernel(ids, w, m, v, sw, sm, sv, out, wide):
    tall, cols = w.shape
    wide[...] = jnp.zeros_like(wide)
    at = lax.broadcasted_iota(jnp.int32, (tall, cols), 0)
    for n, (router, small) in enumerate(((w, sw), (m, sm), (v, sv))):
        values = [
            jnp.sum(jnp.where(at == ids[e], router[...], 0.0), axis=0, keepdims=True)
            for e in range(2)
        ] + [small[i : i + 1, :] for i in range(2)]
        for part, value in enumerate(values):
            lanes = slice(part * cols, (part + 1) * cols)
            top = to_float(to_low(value))
            wide[8 + 2 * n : 9 + 2 * n, lanes] = top
            wide[9 + 2 * n : 10 + 2 * n, lanes] = value - top
    out[...] = to_low(wide[...])


def selected_parts(ids, *values):
    shape = (EXTRA, 512)
    call = kernel(
        parts_kernel,
        [(HELD, shape, jnp.bfloat16)],
        [SCALARS] + [LOCAL] * len(values),
        scratch=[pltpu.VMEM(shape, jnp.float32)],
        name="parts",
        cost=2 * 2**20,
    )
    return call(ids, *values)[0]


def extras_kernel(router, small, out, wide):
    cols, shard = 128, 256
    wide[...] = jnp.zeros_like(wide)
    for x in range(NX):
        for d in range(NZ * NC):
            at = x * NZ * NC + d
            for e in range(2):
                wide[x, d : d + 1, e * cols : (e + 1) * cols] = router[
                    e : e + 1, at * cols : (at + 1) * cols
                ]
            wide[x, d : d + 1, 2 * cols : 2 * cols + shard] = small[
                0:1, at * shard : (at + 1) * shard
            ]
    out[...] = to_low(wide[...])


def pack_extras(router_grads, small_grads):
    feats = 512
    call = kernel(
        extras_kernel,
        [(LOCAL, (NX, EXTRA, feats), jnp.bfloat16)],
        [LOCAL, LOCAL],
        scratch=[pltpu.VMEM((NX, EXTRA, feats), jnp.float32)],
        name="extras",
    )
    return call(router_grads, small_grads)[0]


def both_cores(own, theirs, start, rows):
    at = pl.ds(start, rows)
    return to_float(own[at, :]) + to_float(theirs[at, :])


def pair_kernel(place, own, theirs, extras, *refs):
    outs = refs[-own.shape[0] :]
    for n in range(min(own.shape[0], 2)):
        count = own.shape[1]
        outs[n][:count, :] = to_low(both_cores(own.at[n], theirs.at[n], 0, count))
        outs[n][count:, :] = extras[place[n]]
    if own.shape[0] > 1:
        router, hop = refs[:2]
        outs[2][0] = router[...]
        outs[2][1] = hop[...]


def pair(place, own, theirs, extras, *routers):
    chunks, rows, feats = own.shape
    out = (HELD, (rows + EXTRA, feats), jnp.bfloat16)
    joined = [(HELD, (2, *r.shape), jnp.bfloat16) for r in routers[:1]]
    call = kernel(
        pair_kernel,
        [out] * min(chunks, 2) + joined,
        [SCALARS] + [HELD] * (3 + len(routers)),
        name="pair",
    )
    return call(place, own, theirs, extras, *routers)


def total_kernel(
    place, own, theirs, extras, state, r1, r2, r3, router, hop, mine, s1, s2, s3, routers
):
    routers[:2] = router[...]
    routers[2:] = hop[...]
    _, count, feats = own.shape
    rows = count // (2 * NZ)
    more = to_float(extras[place[0]]) + to_float(state[...])
    for r in (r1, r2, r3):
        more = more + to_float(r[count:, :])
    for j, out in enumerate((mine, s1, s2, s3)):
        zl = lax.rem(place[1] + j, NZ)
        for e in range(2):
            at = pl.multiple_of((e * NZ + zl) * rows, 16)
            total = both_cores(own.at[2], theirs.at[2], at, rows)
            for r in (r1, r2, r3):
                total = total + to_float(r[pl.ds(at, rows), :])
            out[e * rows : (e + 1) * rows, :] = total.astype(out.dtype)
        out[2 * rows :, :] = more.astype(out.dtype)


def total_up(place, own, theirs, extras, state, arrived, router, hop):
    _, count, feats = own.shape
    rows = count // NZ + EXTRA
    call = kernel(
        total_kernel,
        [(HELD, (rows, feats), jnp.bfloat16)] * 4
        + [(HELD, (4, *router.shape[1:]), jnp.bfloat16)],
        [SCALARS] + [HELD] * 9,
        name="total",
    )
    return call(place, own, theirs, extras, state, *arrived, router, hop)


def rate_at(spot, lengths, rate):
    factor = jnp.zeros(spot.shape, jnp.float32)
    begin = jnp.int32(0)
    for k in range(lengths.shape[0]):
        end = begin + lengths[k]
        factor = jnp.where((spot >= begin) & (spot < end), rate[k], factor)
        begin = end
    return factor


def expert_kernel(
    place, lengths, rate, mine, r1, r2, r3, h0, h1, h2, h3, w_far, m_far, v_far, *refs
):
    low, extras, more, routers, w, m, v, sems = refs
    experts, rows, feats = w.shape
    copies = fetch((w_far, m_far, v_far), (w, m, v), sems)
    for k, hop in enumerate((h0, h1, h2, h3)):
        routers[NZ * k : NZ * (k + 1)] = hop[...]

    ix, iz, ic = place[0], place[1], place[2]
    blocks = [to_float(r[experts * rows :, :]) for r in (mine, r1, r2, r3)]
    sums = blocks[0] + blocks[1] + blocks[2] + blocks[3]
    more[...] = sums
    shape = blocks[0].shape
    row = lax.broadcasted_iota(jnp.int32, shape, 0)
    lane = lax.broadcasted_iota(jnp.int32, shape, 1)
    state = [jnp.zeros(shape, jnp.float32) for _ in range(4)]
    for j, block in enumerate(blocks):
        zl = lax.rem(iz - j + NZ, NZ)
        here = row == ix * NZ + zl
        for n in range(3):
            value = block[8 + 2 * n : 9 + 2 * n, :] + block[9 + 2 * n : 10 + 2 * n, :]
            state[n] = jnp.where(here, value, state[n])
        grad = jnp.sum(jnp.where(row == zl * NC + ic, sums, 0.0), axis=0, keepdims=True)
        state[3] = jnp.where(here, grad, state[3])
    half = feats // 2
    spot = (row * NC + ic) * half + lane - half
    factor = jnp.where(lane < half, 1.0, rate_at(spot, lengths, rate))
    decay = jnp.where(lane < half, decay_rate, 0.0)
    extras[...] = to_low(adamw(*state, factor, decay)[0])

    for copy in copies:
        copy.wait()
    for e in range(experts):
        at = slice(e * rows, (e + 1) * rows)
        grad = to_float(mine[at, :]) + to_float(r1[at, :]) + to_float(r2[at, :]) + to_float(r3[at, :])
        low[e] = to_low(adamw(w[e], m[e], v[e], grad, 1.0, decay_rate)[0])


def expert_update(place, lengths, rate, mine, arrived, w, m, v, routers):
    feats = w.shape[2]
    call = kernel(
        expert_kernel,
        [
            (HELD, w.shape, jnp.bfloat16),
            (HELD, (EXTRA, feats), jnp.bfloat16),
            (HELD, (EXTRA, feats), jnp.float32),
            (HELD, (NX * NZ, *routers[0].shape[1:]), jnp.bfloat16),
        ],
        [SCALARS] * 3 + [HELD] * 8 + [FAR] * 3,
        scratch=[pltpu.VMEM(w.shape, jnp.float32)] * 3 + [pltpu.SemaphoreType.DMA((3,))],
        name="expert_update",
    )
    return call(place, lengths, rate, mine, *arrived, *routers, w, m, v)


def others_kernel(place, ids, lengths, rate, more, r1, r2, r3, mine, *refs):
    (ew, em, ev, w, m, v, sw, sm, sv), refs = refs[:9], refs[9:]
    expert_outs, refs = refs[:3], refs[3:]
    new, moment, second, small_new, small_moment, small_second, token, held = refs
    experts, rows, feats = ew.shape
    for e in range(experts):
        at = slice(e * rows, (e + 1) * rows)
        grad = to_float(mine[at, :]) + to_float(r1[at, :]) + to_float(r2[at, :]) + to_float(r3[at, :])
        results = adamw(ew[e], em[e], ev[e], grad, 1.0, decay_rate)
        for out, value in zip(expert_outs, results):
            out[e] = value
    token[...] = jnp.zeros_like(token)
    tall, cols = w.shape
    shard_rows = sw.shape[0]
    rows = lax.broadcasted_iota(jnp.int32, more.shape, 0)
    grad_row = jnp.sum(jnp.where(rows == place[0], more[...], 0.0), axis=0, keepdims=True)
    at = lax.broadcasted_iota(jnp.int32, (tall, cols), 0)
    grad = jnp.zeros((tall, cols), jnp.float32)
    for e in range(ids.shape[0]):
        part = grad_row[:, e * cols : (e + 1) * cols]
        grad = grad + jnp.where(at == ids[e], part, 0.0)
    for i in range(shard_rows):
        part = (ids.shape[0] + i) * cols
        held[i : i + 1, :] = grad_row[:, part : part + cols]
    weight, first, squared = adamw(w[...], m[...], v[...], grad, 1.0, decay_rate)
    new[...] = weight
    moment[...] = first
    second[...] = squared
    spot = (
        place[1]
        + lax.broadcasted_iota(jnp.int32, (shard_rows, cols), 0) * cols
        + lax.broadcasted_iota(jnp.int32, (shard_rows, cols), 1)
    )
    factor = rate_at(spot, lengths, rate)
    weight, first, squared = adamw(
        sw[...], sm[...], sv[...], held[:shard_rows, :], factor, 0.0
    )
    small_new[...] = weight
    small_moment[...] = first
    small_second[...] = squared


def others_update(place, ids, lengths, rate, more, arrived, mine, expert, router, small):
    cols = router[0].shape[1]
    call = kernel(
        others_kernel,
        [(LOCAL, r.shape, jnp.float32) for r in (*expert, *router, *small)]
        + [(HELD, (8, cols), jnp.float32)],
        [SCALARS] * 4 + [HELD] * 4 + [LOCAL] * 10,
        scratch=[pltpu.VMEM((8, cols), jnp.float32)],
        name="others_update",
        cost=4 * 2**20,
    )
    return call(place, ids, lengths, rate, more, *arrived, mine, *expert, *router, *small)


def halve_kernel(place, *refs):
    pieces, (extras, token, out) = refs[:NZ], refs[NZ:]
    experts, rows, feats = pieces[0].shape
    for s in range(NZ):
        for q in range(NZ):

            @pl.when((place[0] ^ q) == s)
            def _():
                for e in range(experts):
                    to = (2 * e + s % 2) * rows
                    lanes = slice((s // 2) * feats, (s // 2 + 1) * feats)
                    out[to : to + rows, lanes] = pieces[q][e]

    out[2 * experts * rows :, :feats] = extras[...]
    out[2 * experts * rows :, feats:] = jnp.zeros((EXTRA, feats), jnp.bfloat16)


def halve(place, pieces, extras, token):
    experts, rows, feats = pieces[0].shape
    call = kernel(
        halve_kernel,
        [
            (HELD, (2 * experts * rows + EXTRA, NH * feats), jnp.bfloat16),
        ],
        [SCALARS] + [HELD] * (NZ + 2),
        name="halve",
    )
    return call(place, *pieces, extras, token)[0]


def lay(place, n, x, piece, out, sems):
    rows, wide = out.shape[3], piece.shape[1]
    at = pl.multiple_of(x * wide, wide)
    copies = []
    for e in range(2):
        for b in range(2):
            part = (2 * e + b) * rows
            copies.append(
                pltpu.make_async_copy(
                    piece.at[part : part + rows, :],
                    out.at[e, b, place[0] ^ n, :, pl.ds(at, wide)],
                    sems.at[len(copies)],
                )
            )
            copies[-1].start()
    return copies


def spread(core, row, d, lines, packed):
    cols = packed.shape[1]
    for e in range(2):
        at = pl.multiple_of(d * cols, cols)
        lines[e : e + 1, pl.ds(at, cols)] = row[:, e * cols : (e + 1) * cols]
    for i in range(2):
        packed[pl.ds(2 * d + i, 1), :] = row[:, (2 + i) * cols : (3 + i) * cols]


def finish_kernel(place, ids, *refs):
    count = 2 * NX
    pieces, routers, refs = refs[:count], refs[count : count + 2], refs[count + 2 :]
    out, patched_far, small, patched, lines, packed, out_sems, sem = refs
    cols = packed.shape[1]
    copies = []
    for n, piece in enumerate(pieces):
        copies += lay(place, n % 2, place[1 + n // 2], piece, out, out_sems.at[n])
    for n, blocks in enumerate(routers):
        for x in range(NX):
            for z in range(NZ):
                d = ((place[5] ^ x) * NZ + (place[6] ^ z)) * NC + (place[0] ^ n)
                at = pl.ds(pl.multiple_of(d * cols, cols), cols)
                patched[:, at] = blocks[x * NZ + z]
    for n in range(2):
        core = place[0] ^ n
        extras = sum(to_float(p[p.shape[0] - EXTRA :, : p.shape[1] // NH]) for p in pieces[n::2])
        for r in range(NX * NZ):
            spread(core, extras[r : r + 1, :], r * NC + core, lines, packed)
    spot = lax.broadcasted_iota(jnp.int32, (16, patched.shape[1]), 0)
    for n in range(2):
        at = pl.multiple_of(lax.div(ids[n], 16) * 16, 16)
        value = to_float(patched[pl.ds(at, 16), :])
        value = jnp.where(spot + at == ids[n], lines[n : n + 1, :], value)
        patched[pl.ds(at, 16), :] = to_low(value)
    move = pltpu.make_async_copy(patched, patched_far, sem)
    move.start()
    small[...] = to_low(packed[...])
    for copy in copies:
        copy.wait()
    move.wait()


def finish(place, ids, pieces, routers):
    rows, wide = pieces[0].shape
    n_dp = NX * NZ * NC
    tall, cols = routers[0].shape[1:]
    call = kernel(
        finish_kernel,
        [
            (FAR, (2, 2, NC, (rows - EXTRA) // 4, NY * wide), jnp.bfloat16),
            (FAR, (tall, n_dp * cols), jnp.bfloat16),
            (LOCAL, (2 * n_dp, cols), jnp.bfloat16),
        ],
        [SCALARS] * 2 + [HELD] * (len(pieces) + len(routers)),
        scratch=[
            pltpu.VMEM((tall, n_dp * cols), jnp.bfloat16),
            pltpu.VMEM((2, n_dp * cols), jnp.float32),
            pltpu.VMEM((2 * n_dp, cols), jnp.float32),
            pltpu.SemaphoreType.DMA((len(pieces), 4)),
            pltpu.SemaphoreType.DMA,
        ],
        name="finish",
    )
    return call(place, ids, *pieces, *routers)


def body(
    hidden_act,
    out_grad,
    router_grads,
    small_grads,
    expert_ids,
    small_lengths,
    small_rate,
    expert_w,
    expert_m,
    expert_v,
    router_w,
    router_m,
    router_v,
    small_w,
    small_m,
    small_v,
):
    ix, iy, iz, ic = (lax.axis_index(name) for name in ("x", "y", "zl", "core"))
    dp_index = (ix * NZ + iz) * NC + ic
    shard_len = small_w.shape[0]

    opposite, above, below = ((ix + k) % NX for k in (2, 1, 3))
    far_own, far_send, own, send = product(
        numbers(ic, opposite, above, below, ix), hidden_act, out_grad
    )

    zero = jnp.zeros_like(router_w)
    router = adamw(after(router_w, far_send), router_m, router_v, zero, 1.0, decay_rate)[0]
    router = to_low(router)

    extras = pack_extras(after(router_grads[0], far_send), small_grads)
    extras = to_low(to_float(extras) + to_float(swap_core(extras)))
    sent = list(pair(numbers(opposite), far_own, swap_core(far_send), extras))
    theirs = swap_core(send)
    hop = swap_with(router, "zl", NZ, 1)
    *near, router = pair(numbers(above, below), own, theirs, extras, router, hop)
    sent += near
    arrived = [shift(value, "x", NX, k) for k, value in zip((2, 1, 3), sent)]
    router_state = (router_w, router_m, router_v)
    small_state = [s.reshape(-1, 128) for s in (small_w, small_m, small_v)]
    parts = selected_parts(expert_ids, *router_state, *small_state)
    hop = swap_with(router, "zl", NZ, 2)
    mine, *sends, router = total_up(
        numbers(ix, iz), own, theirs, extras, parts, arrived, router, hop
    )
    routers = [router] + [swap_with(router, "x", NX, k) for k in (1, 2, 3)]
    arrived = [shift(send, "zl", NZ, j + 1) for j, send in enumerate(sends)]
    expert_state = (expert_w, expert_m, expert_v)
    low, extras, more, router = expert_update(
        numbers(ix, iz, ic), small_lengths, small_rate, mine, arrived, *expert_state, routers
    )
    others = others_update(
        numbers(iz * NC + ic, dp_index * shard_len),
        expert_ids,
        small_lengths,
        small_rate,
        more,
        arrived,
        mine,
        expert_state,
        router_state,
        small_state,
    )
    new_expert, expert_moment, expert_second = others[:3]
    new_router, router_moment, router_second = others[3:6]
    new_small, small_moment, small_second = (s.reshape(-1) for s in others[6:9])

    first, second = (lax.ppermute(low, AXES, to_owner_group(q)) for q in (0, 2))
    pieces = [first, swap_with(first, "zl", NZ, 1), second, swap_with(second, "zl", NZ, 1)]
    half = halve(numbers(iz), pieces, extras, others[9])
    pieces = []
    for k in (0, 1, 3, 2):
        piece = shift(half, "x", NX, k) if k else half
        pieces += [piece, swap_core(piece)]
    places = [(ix - iy - k) % NX for k in (0, 1, 3, 2)]
    whole, router_rollout, small_rollout = finish(
        numbers(ic, *places, ix, iz), expert_ids, pieces, [router, swap_core(router)]
    )
    expert_rollout = whole.reshape(whole.shape[0], -1, whole.shape[-1])
    small_rollout = small_rollout.reshape(-1)
    return (
        new_expert,
        expert_moment,
        expert_second,
        new_router,
        router_moment,
        router_second,
        new_small,
        small_moment,
        small_second,
        expert_rollout,
        router_rollout,
        small_rollout,
    )


def solution(mesh):
    fine = Mesh(mesh.devices.reshape(SIZES), AXES)
    placed = (
        P(DP, None, None),
        P(DP, None, GROUP),
        P(DP, None, None),
        P(DP, None),
        P(),
        P(),
        P(),
        P(None, DP, GROUP),
        P(None, DP, GROUP),
        P(None, DP, GROUP),
        P(None, DP),
        P(None, DP),
        P(None, DP),
        P(DP),
        P(DP),
        P(DP),
    )
    return jax.shard_map(
        body,
        mesh=fine,
        in_specs=placed,
        out_specs=(
            P(None, DP, GROUP),
            P(None, DP, GROUP),
            P(None, DP, GROUP),
            P(None, DP),
            P(None, DP),
            P(None, DP),
            P(DP),
            P(DP),
            P(DP),
            P(None, GROUP, None),
            P(),
            P(),
        ),
        check_vma=False,
    )
```

```python
import jax
import jax.numpy as jnp
from jax import lax
from jax.experimental import pallas as pl
from jax.experimental.pallas import tpu as pltpu
from jax.sharding import Mesh, PartitionSpec as P

beta_one = 0.9
beta_two = 0.95
learn_rate = 0.1
decay_rate = 0.1
eps = 1e-08
adam_step = 12

AXES = ("x", "zl", "core", "y", "zh")
SIZES = (4, 4, 2, 4, 2)
DP = AXES[:3]
GROUP = AXES[3:]
NX, NZ, NC, NY, NH = SIZES
EXTRA = 16

SCALARS = pl.BlockSpec(memory_space=pltpu.SMEM)
LOCAL = pl.BlockSpec(memory_space=pltpu.VMEM)
HELD = pl.BlockSpec(memory_space=pltpu.VMEM)
FAR = pl.BlockSpec(memory_space=pltpu.HBM)


def adamw(weight, moment, second, grad, factor, decay):
    moment_new = beta_one * moment + (1.0 - beta_one) * grad
    second_new = beta_two * second + (1.0 - beta_two) * grad * grad
    corrected = moment_new / (1.0 - beta_one**adam_step)
    scaled = second_new / (1.0 - beta_two**adam_step)
    weight_new = weight - learn_rate * factor * (
        corrected / (jnp.sqrt(scaled) + eps) + decay * weight
    )
    return (weight_new, moment_new, second_new)


def shift(value, axis, size, step):
    return lax.ppermute(value, axis, [(i, (i + step) % size) for i in range(size)])


def swap_with(value, axis, size, step):
    return lax.ppermute(value, axis, [(i, i ^ step) for i in range(size)])


def swap_core(value):
    return lax.ppermute(value, "core", [(0, 1), (1, 0)])


def flat(x, zl, core, y, zh):
    return (((x * NZ + zl) * NC + core) * NY + y) * NH + zh


def to_owner_group(step):
    pairs = []
    for x in range(NX):
        for zl in range(NZ):
            a, b = zl // 2, zl % 2
            for core in range(NC):
                for y in range(NY):
                    for zh in range(NH):
                        to = flat((x + y) % NX, (2 * zh + b) ^ step, core, x, a)
                        pairs.append((flat(x, zl, core, y, zh), to))
    return pairs


def after(value, *others):
    return lax.optimization_barrier((value,) + others)[0]


def to_float(value):
    return value.astype(jnp.float32)


def to_low(value):
    return value.astype(jnp.bfloat16)


def numbers(*values):
    return jnp.stack([jnp.asarray(v, jnp.int32) for v in values])


def kernel(body, outs, ins, scratch=(), aliases=None, name=None, cost=0, room=16):
    shapes = []
    for spec, shape, dtype in outs:
        if spec is HELD:
            shapes.append(pltpu.VMEM(shape, dtype))
        else:
            shapes.append(jax.ShapeDtypeStruct(shape, dtype))
    call = pl.pallas_call(
        body,
        out_shape=shapes,
        in_specs=ins,
        out_specs=[spec for spec, _, _ in outs],
        scratch_shapes=list(scratch),
        input_output_aliases=aliases or {},
        cost_estimate=pl.CostEstimate(flops=0, bytes_accessed=cost, transcendentals=0),
        compiler_params=pltpu.CompilerParams(vmem_limit_bytes=room * 2**20),
        name=name,
    )

    def run(*values):
        placed = []
        for spec, value in zip(ins, values):
            if spec is HELD:
                value = pltpu.with_memory_space_constraint(value, pltpu.VMEM)
            elif spec is FAR:
                value = pltpu.with_memory_space_constraint(value, pltpu.HBM)
            placed.append(value)
        return call(*placed)

    return run


def fetch(sources, targets, sems):
    copies = [
        pltpu.make_async_copy(a, b, sems.at[n]) for n, (a, b) in enumerate(zip(sources, targets))
    ]
    for copy in copies:
        copy.start()
    return copies


def product_kernel(place, hidden, grads_far, far_keep, far_send, keep, send, *scratch):
    raw, grads, left, right, sems = scratch
    tokens, experts, wide = hidden.shape
    wide = wide // NX
    rows = wide // (NZ * NC)
    blocks = sems.shape[0] - 1
    spans = [pl.ds(p * (tokens // blocks), tokens // blocks) for p in range(blocks)]
    copies = fetch(
        [grads_far] + [hidden.at[at] for at in spans], [grads] + [raw.at[at] for at in spans], sems
    )
    copies[0].wait()
    for at, copy in zip(spans, copies[1:]):
        right[:, at, :] = jnp.swapaxes(grads[at], 0, 1)
        copy.wait()
        left[:, at, :] = jnp.swapaxes(raw[at], 0, 1)
    for n in range(NX):
        at = pl.multiple_of(place[1 + n] * wide, 128)
        for e in range(experts):
            value = lax.dot_general(
                left[e, :, pl.ds(at, wide)],
                right[e],
                (((0,), (0,)), ((), ())),
                preferred_element_type=jnp.float32,
            )
            mine, other = (far_keep, far_send) if n == 0 else (keep, send)
            m = max(n - 1, 0)
            for zl in range(NZ):
                first = value[2 * zl * rows : (2 * zl + 1) * rows, :]
                second = value[(2 * zl + 1) * rows : (2 * zl + 2) * rows, :]
                to = (e * NZ + zl) * rows
                mine[m, to : to + rows, :] = to_low(jnp.where(place[0] == 0, first, second))
                other[m, to : to + rows, :] = to_low(jnp.where(place[0] == 0, second, first))


def product(place, hidden_act, out_grad):
    tokens, experts, hidden = hidden_act.shape
    feats = out_grad.shape[2]
    rows = experts * hidden // NX // NC
    one, rest = (1, rows, feats), (NX - 1, rows, feats)
    call = kernel(
        product_kernel,
        [(HELD, shape, jnp.bfloat16) for shape in (one, one, rest, rest)],
        [SCALARS, FAR, FAR],
        scratch=[
            pltpu.VMEM(hidden_act.shape, jnp.bfloat16),
            pltpu.VMEM(out_grad.shape, jnp.bfloat16),
            pltpu.VMEM((experts, tokens, hidden), jnp.bfloat16),
            pltpu.VMEM((experts, tokens, feats), jnp.bfloat16),
            pltpu.SemaphoreType.DMA((5,)),
        ],
        name="product",
        room=40,
    )
    return call(place, hidden_act, out_grad)


def parts_kernel(ids, w, m, v, sw, sm, sv, out, wide):
    tall, cols = w.shape
    wide[...] = jnp.zeros_like(wide)
    at = lax.broadcasted_iota(jnp.int32, (tall, cols), 0)
    for n, (router, small) in enumerate(((w, sw), (m, sm), (v, sv))):
        values = [
            jnp.sum(jnp.where(at == ids[e], router[...], 0.0), axis=0, keepdims=True)
            for e in range(2)
        ] + [small[i : i + 1, :] for i in range(2)]
        for part, value in enumerate(values):
            lanes = slice(part * cols, (part + 1) * cols)
            top = to_float(to_low(value))
            wide[8 + 2 * n : 9 + 2 * n, lanes] = top
            wide[9 + 2 * n : 10 + 2 * n, lanes] = value - top
    out[...] = to_low(wide[...])


def selected_parts(ids, *values):
    shape = (EXTRA, 512)
    call = kernel(
        parts_kernel,
        [(HELD, shape, jnp.bfloat16)],
        [SCALARS] + [LOCAL] * len(values),
        scratch=[pltpu.VMEM(shape, jnp.float32)],
        name="parts",
        cost=2 * 2**20,
    )
    return call(ids, *values)[0]


def extras_kernel(router, small, out, wide):
    cols, shard = 128, 256
    wide[...] = jnp.zeros_like(wide)
    for x in range(NX):
        for d in range(NZ * NC):
            at = x * NZ * NC + d
            for e in range(2):
                wide[x, d : d + 1, e * cols : (e + 1) * cols] = router[
                    e : e + 1, at * cols : (at + 1) * cols
                ]
            wide[x, d : d + 1, 2 * cols : 2 * cols + shard] = small[
                0:1, at * shard : (at + 1) * shard
            ]
    out[...] = to_low(wide[...])


def pack_extras(router_grads, small_grads):
    feats = 512
    call = kernel(
        extras_kernel,
        [(LOCAL, (NX, EXTRA, feats), jnp.bfloat16)],
        [LOCAL, LOCAL],
        scratch=[pltpu.VMEM((NX, EXTRA, feats), jnp.float32)],
        name="extras",
    )
    return call(router_grads, small_grads)[0]


def both_cores(own, theirs, start, rows):
    at = pl.ds(start, rows)
    return to_float(own[at, :]) + to_float(theirs[at, :])


def pair_kernel(place, own, theirs, extras, *refs):
    outs = refs[-own.shape[0] :]
    for n in range(min(own.shape[0], 2)):
        count = own.shape[1]
        outs[n][:count, :] = to_low(both_cores(own.at[n], theirs.at[n], 0, count))
        outs[n][count:, :] = extras[place[n]]
    if own.shape[0] > 1:
        router, hop = refs[:2]
        outs[2][0] = router[...]
        outs[2][1] = hop[...]


def pair(place, own, theirs, extras, *routers):
    chunks, rows, feats = own.shape
    out = (HELD, (rows + EXTRA, feats), jnp.bfloat16)
    joined = [(HELD, (2, *r.shape), jnp.bfloat16) for r in routers[:1]]
    call = kernel(
        pair_kernel,
        [out] * min(chunks, 2) + joined,
        [SCALARS] + [HELD] * (3 + len(routers)),
        name="pair",
    )
    return call(place, own, theirs, extras, *routers)


def total_kernel(
    place, own, theirs, extras, state, r1, r2, r3, router, hop, mine, s1, s2, s3, routers
):
    routers[:2] = router[...]
    routers[2:] = hop[...]
    _, count, feats = own.shape
    rows = count // (2 * NZ)
    more = to_float(extras[place[0]]) + to_float(state[...])
    for r in (r1, r2, r3):
        more = more + to_float(r[count:, :])
    for j, out in enumerate((mine, s1, s2, s3)):
        zl = lax.rem(place[1] + j, NZ)
        for e in range(2):
            at = pl.multiple_of((e * NZ + zl) * rows, 16)
            total = both_cores(own.at[2], theirs.at[2], at, rows)
            for r in (r1, r2, r3):
                total = total + to_float(r[pl.ds(at, rows), :])
            out[e * rows : (e + 1) * rows, :] = total.astype(out.dtype)
        out[2 * rows :, :] = more.astype(out.dtype)


def total_up(place, own, theirs, extras, state, arrived, router, hop):
    _, count, feats = own.shape
    rows = count // NZ + EXTRA
    call = kernel(
        total_kernel,
        [(HELD, (rows, feats), jnp.bfloat16)] * 4
        + [(HELD, (4, *router.shape[1:]), jnp.bfloat16)],
        [SCALARS] + [HELD] * 9,
        name="total",
    )
    return call(place, own, theirs, extras, state, *arrived, router, hop)


def rate_at(spot, lengths, rate):
    factor = jnp.zeros(spot.shape, jnp.float32)
    begin = jnp.int32(0)
    for k in range(lengths.shape[0]):
        end = begin + lengths[k]
        factor = jnp.where((spot >= begin) & (spot < end), rate[k], factor)
        begin = end
    return factor


def expert_kernel(
    place, lengths, rate, mine, r1, r2, r3, h0, h1, h2, h3, w_far, m_far, v_far, *refs
):
    low, extras, more, routers, w, m, v, sems = refs
    experts, rows, feats = w.shape
    copies = fetch((w_far, m_far, v_far), (w, m, v), sems)
    for k, hop in enumerate((h0, h1, h2, h3)):
        routers[NZ * k : NZ * (k + 1)] = hop[...]

    ix, iz, ic = place[0], place[1], place[2]
    blocks = [to_float(r[experts * rows :, :]) for r in (mine, r1, r2, r3)]
    sums = blocks[0] + blocks[1] + blocks[2] + blocks[3]
    more[...] = sums
    shape = blocks[0].shape
    row = lax.broadcasted_iota(jnp.int32, shape, 0)
    lane = lax.broadcasted_iota(jnp.int32, shape, 1)
    state = [jnp.zeros(shape, jnp.float32) for _ in range(4)]
    for j, block in enumerate(blocks):
        zl = lax.rem(iz - j + NZ, NZ)
        here = row == ix * NZ + zl
        for n in range(3):
            value = block[8 + 2 * n : 9 + 2 * n, :] + block[9 + 2 * n : 10 + 2 * n, :]
            state[n] = jnp.where(here, value, state[n])
        grad = jnp.sum(jnp.where(row == zl * NC + ic, sums, 0.0), axis=0, keepdims=True)
        state[3] = jnp.where(here, grad, state[3])
    half = feats // 2
    spot = (row * NC + ic) * half + lane - half
    factor = jnp.where(lane < half, 1.0, rate_at(spot, lengths, rate))
    decay = jnp.where(lane < half, decay_rate, 0.0)
    extras[...] = to_low(adamw(*state, factor, decay)[0])

    for copy in copies:
        copy.wait()
    for e in range(experts):
        at = slice(e * rows, (e + 1) * rows)
        grad = to_float(mine[at, :]) + to_float(r1[at, :]) + to_float(r2[at, :]) + to_float(r3[at, :])
        low[e] = to_low(adamw(w[e], m[e], v[e], grad, 1.0, decay_rate)[0])


def expert_update(place, lengths, rate, mine, arrived, w, m, v, routers):
    feats = w.shape[2]
    call = kernel(
        expert_kernel,
        [
            (HELD, w.shape, jnp.bfloat16),
            (HELD, (EXTRA, feats), jnp.bfloat16),
            (HELD, (EXTRA, feats), jnp.float32),
            (HELD, (NX * NZ, *routers[0].shape[1:]), jnp.bfloat16),
        ],
        [SCALARS] * 3 + [HELD] * 8 + [FAR] * 3,
        scratch=[pltpu.VMEM(w.shape, jnp.float32)] * 3 + [pltpu.SemaphoreType.DMA((3,))],
        name="expert_update",
    )
    return call(place, lengths, rate, mine, *arrived, *routers, w, m, v)


def others_kernel(place, ids, lengths, rate, more, r1, r2, r3, mine, *refs):
    (ew, em, ev, w, m, v, sw, sm, sv), refs = refs[:9], refs[9:]
    expert_outs, refs = refs[:3], refs[3:]
    new, moment, second, small_new, small_moment, small_second, token, held = refs
    experts, rows, feats = ew.shape
    for e in range(experts):
        at = slice(e * rows, (e + 1) * rows)
        grad = to_float(mine[at, :]) + to_float(r1[at, :]) + to_float(r2[at, :]) + to_float(r3[at, :])
        results = adamw(ew[e], em[e], ev[e], grad, 1.0, decay_rate)
        for out, value in zip(expert_outs, results):
            out[e] = value
    token[...] = jnp.zeros_like(token)
    tall, cols = w.shape
    shard_rows = sw.shape[0]
    rows = lax.broadcasted_iota(jnp.int32, more.shape, 0)
    grad_row = jnp.sum(jnp.where(rows == place[0], more[...], 0.0), axis=0, keepdims=True)
    at = lax.broadcasted_iota(jnp.int32, (tall, cols), 0)
    grad = jnp.zeros((tall, cols), jnp.float32)
    for e in range(ids.shape[0]):
        part = grad_row[:, e * cols : (e + 1) * cols]
        grad = grad + jnp.where(at == ids[e], part, 0.0)
    for i in range(shard_rows):
        part = (ids.shape[0] + i) * cols
        held[i : i + 1, :] = grad_row[:, part : part + cols]
    weight, first, squared = adamw(w[...], m[...], v[...], grad, 1.0, decay_rate)
    new[...] = weight
    moment[...] = first
    second[...] = squared
    spot = (
        place[1]
        + lax.broadcasted_iota(jnp.int32, (shard_rows, cols), 0) * cols
        + lax.broadcasted_iota(jnp.int32, (shard_rows, cols), 1)
    )
    factor = rate_at(spot, lengths, rate)
    weight, first, squared = adamw(
        sw[...], sm[...], sv[...], held[:shard_rows, :], factor, 0.0
    )
    small_new[...] = weight
    small_moment[...] = first
    small_second[...] = squared


def others_update(place, ids, lengths, rate, more, arrived, mine, expert, router, small):
    cols = router[0].shape[1]
    call = kernel(
        others_kernel,
        [(LOCAL, r.shape, jnp.float32) for r in (*expert, *router, *small)]
        + [(HELD, (8, cols), jnp.float32)],
        [SCALARS] * 4 + [HELD] * 4 + [LOCAL] * 10,
        scratch=[pltpu.VMEM((8, cols), jnp.float32)],
        name="others_update",
        cost=4 * 2**20,
    )
    return call(place, ids, lengths, rate, more, *arrived, mine, *expert, *router, *small)


def halve_kernel(place, *refs):
    pieces, (extras, token, out) = refs[:NZ], refs[NZ:]
    experts, rows, feats = pieces[0].shape
    for s in range(NZ):
        for q in range(NZ):

            @pl.when((place[0] ^ q) == s)
            def _():
                for e in range(experts):
                    to = (2 * e + s % 2) * rows
                    lanes = slice((s // 2) * feats, (s // 2 + 1) * feats)
                    out[to : to + rows, lanes] = pieces[q][e]

    out[2 * experts * rows :, :feats] = extras[...]
    out[2 * experts * rows :, feats:] = jnp.zeros((EXTRA, feats), jnp.bfloat16)


def halve(place, pieces, extras, token):
    experts, rows, feats = pieces[0].shape
    call = kernel(
        halve_kernel,
        [
            (HELD, (2 * experts * rows + EXTRA, NH * feats), jnp.bfloat16),
        ],
        [SCALARS] + [HELD] * (NZ + 2),
        name="halve",
    )
    return call(place, *pieces, extras, token)[0]


def lay(place, n, x, piece, out, sems):
    rows, wide = out.shape[3], piece.shape[1]
    at = pl.multiple_of(x * wide, wide)
    copies = []
    for e in range(2):
        for b in range(2):
            part = (2 * e + b) * rows
            copies.append(
                pltpu.make_async_copy(
                    piece.at[part : part + rows, :],
                    out.at[e, b, place[0] ^ n, :, pl.ds(at, wide)],
                    sems.at[len(copies)],
                )
            )
            copies[-1].start()
    return copies


def spread(core, row, d, lines, packed):
    cols = packed.shape[1]
    for e in range(2):
        at = pl.multiple_of(d * cols, cols)
        lines[e : e + 1, pl.ds(at, cols)] = row[:, e * cols : (e + 1) * cols]
    for i in range(2):
        packed[pl.ds(2 * d + i, 1), :] = row[:, (2 + i) * cols : (3 + i) * cols]


def finish_kernel(place, ids, *refs):
    count = 2 * NX
    pieces, routers, refs = refs[:count], refs[count : count + 2], refs[count + 2 :]
    out, patched_far, small, patched, lines, packed, out_sems, sem = refs
    cols = packed.shape[1]
    copies = []
    for n, piece in enumerate(pieces):
        copies += lay(place, n % 2, place[1 + n // 2], piece, out, out_sems.at[n])
    for n, blocks in enumerate(routers):
        for x in range(NX):
            for z in range(NZ):
                d = ((place[5] ^ x) * NZ + (place[6] ^ z)) * NC + (place[0] ^ n)
                at = pl.ds(pl.multiple_of(d * cols, cols), cols)
                patched[:, at] = blocks[x * NZ + z]
    for n in range(2):
        core = place[0] ^ n
        extras = sum(to_float(p[p.shape[0] - EXTRA :, : p.shape[1] // NH]) for p in pieces[n::2])
        for r in range(NX * NZ):
            spread(core, extras[r : r + 1, :], r * NC + core, lines, packed)
    spot = lax.broadcasted_iota(jnp.int32, (16, patched.shape[1]), 0)
    for n in range(2):
        at = pl.multiple_of(lax.div(ids[n], 16) * 16, 16)
        value = to_float(patched[pl.ds(at, 16), :])
        value = jnp.where(spot + at == ids[n], lines[n : n + 1, :], value)
        patched[pl.ds(at, 16), :] = to_low(value)
    move = pltpu.make_async_copy(patched, patched_far, sem)
    move.start()
    small[...] = to_low(packed[...])
    for copy in copies:
        copy.wait()
    move.wait()


def finish(place, ids, pieces, routers):
    rows, wide = pieces[0].shape
    n_dp = NX * NZ * NC
    tall, cols = routers[0].shape[1:]
    call = kernel(
        finish_kernel,
        [
            (FAR, (2, 2, NC, (rows - EXTRA) // 4, NY * wide), jnp.bfloat16),
            (FAR, (tall, n_dp * cols), jnp.bfloat16),
            (LOCAL, (2 * n_dp, cols), jnp.bfloat16),
        ],
        [SCALARS] * 2 + [HELD] * (len(pieces) + len(routers)),
        scratch=[
            pltpu.VMEM((tall, n_dp * cols), jnp.bfloat16),
            pltpu.VMEM((2, n_dp * cols), jnp.float32),
            pltpu.VMEM((2 * n_dp, cols), jnp.float32),
            pltpu.SemaphoreType.DMA((len(pieces), 4)),
            pltpu.SemaphoreType.DMA,
        ],
        name="finish",
    )
    return call(place, ids, *pieces, *routers)


def body(
    hidden_act,
    out_grad,
    router_grads,
    small_grads,
    expert_ids,
    small_lengths,
    small_rate,
    expert_w,
    expert_m,
    expert_v,
    router_w,
    router_m,
    router_v,
    small_w,
    small_m,
    small_v,
):
    ix, iy, iz, ic = (lax.axis_index(name) for name in ("x", "y", "zl", "core"))
    dp_index = (ix * NZ + iz) * NC + ic
    shard_len = small_w.shape[0]

    opposite, above, below = (ix ^ k for k in (2, 1, 3))
    far_own, far_send, own, send = product(
        numbers(ic, opposite, above, below, ix), hidden_act, out_grad
    )

    zero = jnp.zeros_like(router_w)
    router = adamw(after(router_w, far_send), router_m, router_v, zero, 1.0, decay_rate)[0]
    router = to_low(router)

    extras = pack_extras(after(router_grads[0], far_send), small_grads)
    extras = to_low(to_float(extras) + to_float(swap_core(extras)))
    sent = list(pair(numbers(opposite), far_own, swap_core(far_send), extras))
    theirs = swap_core(send)
    hop = swap_with(router, "zl", NZ, 1)
    *near, router = pair(numbers(above, below), own, theirs, extras, router, hop)
    sent += near
    arrived = [swap_with(value, "x", NX, k) for k, value in zip((2, 1, 3), sent)]
    router_state = (router_w, router_m, router_v)
    small_state = [s.reshape(-1, 128) for s in (small_w, small_m, small_v)]
    parts = selected_parts(expert_ids, *router_state, *small_state)
    hop = swap_with(router, "zl", NZ, 2)
    mine, *sends, router = total_up(
        numbers(ix, iz), own, theirs, extras, parts, arrived, router, hop
    )
    routers = [router] + [swap_with(router, "x", NX, k) for k in (1, 2, 3)]
    arrived = [shift(send, "zl", NZ, j + 1) for j, send in enumerate(sends)]
    expert_state = (expert_w, expert_m, expert_v)
    low, extras, more, router = expert_update(
        numbers(ix, iz, ic), small_lengths, small_rate, mine, arrived, *expert_state, routers
    )
    others = others_update(
        numbers(iz * NC + ic, dp_index * shard_len),
        expert_ids,
        small_lengths,
        small_rate,
        more,
        arrived,
        mine,
        expert_state,
        router_state,
        small_state,
    )
    new_expert, expert_moment, expert_second = others[:3]
    new_router, router_moment, router_second = others[3:6]
    new_small, small_moment, small_second = (s.reshape(-1) for s in others[6:9])

    first, second = (lax.ppermute(low, AXES, to_owner_group(q)) for q in (0, 2))
    pieces = [first, swap_with(first, "zl", NZ, 1), second, swap_with(second, "zl", NZ, 1)]
    half = halve(numbers(iz), pieces, extras, others[9])
    pieces = []
    for k in (0, 1, 3, 2):
        piece = shift(half, "x", NX, k) if k else half
        pieces += [piece, swap_core(piece)]
    places = [(ix - iy - k) % NX for k in (0, 1, 3, 2)]
    whole, router_rollout, small_rollout = finish(
        numbers(ic, *places, ix, iz), expert_ids, pieces, [router, swap_core(router)]
    )
    expert_rollout = whole.reshape(whole.shape[0], -1, whole.shape[-1])
    small_rollout = small_rollout.reshape(-1)
    return (
        new_expert,
        expert_moment,
        expert_second,
        new_router,
        router_moment,
        router_second,
        new_small,
        small_moment,
        small_second,
        expert_rollout,
        router_rollout,
        small_rollout,
    )


def solution(mesh):
    fine = Mesh(mesh.devices.reshape(SIZES), AXES)
    placed = (
        P(DP, None, None),
        P(DP, None, GROUP),
        P(DP, None, None),
        P(DP, None),
        P(),
        P(),
        P(),
        P(None, DP, GROUP),
        P(None, DP, GROUP),
        P(None, DP, GROUP),
        P(None, DP),
        P(None, DP),
        P(None, DP),
        P(DP),
        P(DP),
        P(DP),
    )
    return jax.shard_map(
        body,
        mesh=fine,
        in_specs=placed,
        out_specs=(
            P(None, DP, GROUP),
            P(None, DP, GROUP),
            P(None, DP, GROUP),
            P(None, DP),
            P(None, DP),
            P(None, DP),
            P(DP),
            P(DP),
            P(DP),
            P(None, GROUP, None),
            P(),
            P(),
        ),
        check_vma=False,
    )
```
